32 devices in a mesh: dom: 16 (over z, y, x), feat: 2 (over core).
Axes of the slice: x: 2, y: 2, z: 4, core: 2. Of those that a mesh axis runs over, the one named last changes fastest.
Arguments:
- history: bfloat16 [16384, 256], P('dom', 'feat'), may hold values from -6 to 6
- pull_list: int32 [16, 16, 2], P('dom'), may hold values from -1 to 7, as said below
- remote_tiles: bfloat16 [16, 16, 2, 128, 128], P('dom'), may hold values from -0.1875 to 0.1875
- remote_dst: int32 [16, 16, 2], P('dom'), may hold values from 0 to 15
- local_tiles: bfloat16 [1024, 128, 128], P('dom'), may hold values from -0.1875 to 0.1875
- local_src: int32 [16, 64], P('dom'), may hold values from 0 to 7
- local_dst: int32 [16, 64], P('dom'), may hold values from 0 to 15
- weight: bfloat16 [256, 256], P(None, 'feat'), may hold values from -0.375 to 0.375
- bias: float32 [256], P('feat'), may hold values from -3 to 3
- cotangent: bfloat16 [16384, 256], P('dom', 'feat'), may hold values from -0.046875 to 0.046875
Outputs:
- new_rows: bfloat16 [16384, 256], P('dom', 'feat')
- grad_weight: float32 [256, 256], P(None, 'feat')
- grad_bias: float32 [256], P('feat')
The draws below stay inside these ranges and needn't reach their ends.
Inputs may be any that keep to these rules, and one draw needn't show every extreme that they name: pull_list[r, o, c] is -1 or a block index local to owner o; in each (r, o) the used entries come first and are distinct; pull_list[r, r] is all -1; every other (r, o) asks 2 or 1 blocks; every partition asks 2 blocks of the next partition, and some owner is asked for 2 blocks by every other partition.
All inputs are finite; a program needn't handle non-finite values.
Results may differ from the reference program's by a relative error of at most 0.0065.
Values may be sent and summed in bfloat16 or wider, within the bound.
No kernel may reach another device: no remote copies, remote signals or barrier semaphores. Data moves between devices by JAX's collectives and lax.ppermute only.
A program may use at most 128 MiB of HBM per device.

```python
import jax
import jax.numpy as jnp
from jax import lax

F = 256
BLK = 128
CAP = 2
NB = 8
NL = 64
NODES = 16384
LTILES = 1024
N_DOM = 16


def draw_pull_list(key, part):
    key_a, key_c, key_d = jax.random.split(key, 3)
    dropped = jax.random.randint(key_a, (N_DOM, N_DOM), 0, 16) == 0
    counts = jnp.where(dropped, CAP - 1, CAP)
    requester = jnp.arange(N_DOM, dtype=jnp.int32)[:, None]
    owner = jnp.arange(N_DOM, dtype=jnp.int32)[None, :]
    full_owner = jax.random.randint(key_c, (), 0, N_DOM)
    counts = jnp.where(owner == full_owner, CAP, counts)
    counts = jnp.where(owner == (requester + 1) % N_DOM, CAP, counts)
    counts = jnp.where(owner == requester, 0, counts)
    offset = jax.random.randint(key_d, (N_DOM, N_DOM), 0, NB)
    slot_ids = jnp.arange(CAP, dtype=jnp.int32)
    chosen = (offset[:, :, None] + slot_ids[None, None, :]) % NB
    return jnp.where(slot_ids[None, None, :] < counts[:, :, None], chosen, -1).astype(jnp.int32)


def with_ends(drawn, key, low, high):
    extent = drawn.shape
    spot = [jax.random.randint(jax.random.fold_in(key, axis), (), 0, extent[axis]) for axis in range(len(extent))]
    drawn = drawn.at[tuple(spot)].set(low)
    longest = extent.index(max(extent))
    spot[longest] = (spot[longest] + 1) % extent[longest]
    return drawn.at[tuple(spot)].set(high)


def shard_levels(key, extent, pieces, low, top_value):
    loudness = 1.0
    for axis_at, blocks in pieces:
        draws = jax.random.uniform(jax.random.fold_in(jax.random.fold_in(key, 6), axis_at), (blocks,), jnp.float32, low / len(pieces), top_value / len(pieces))
        loudness = loudness * jnp.repeat(jnp.exp(draws), extent[axis_at] // blocks).reshape((-1,) + (1,) * (len(extent) - 1 - axis_at))
    return loudness


def centred(own_key, shape, spread, reach, pieces=(), held_as=jnp.bfloat16):
    array = jax.random.normal(own_key, shape, jnp.float32) * spread
    if len(pieces) > 0:
        array = shard_levels(own_key, shape, pieces, -0.22, 0.18) * array
    return jnp.clip(array, min=-reach, max=reach).astype(held_as)


def setup_inputs(seed: int = 0) -> dict:
    streams_of = jax.random.split(jax.random.key(seed), 11)
    history = centred(streams_of[0], (NODES, F), 1.0, 6.0, ((0, 16), (1, 2)))
    pull_list = draw_pull_list(jax.random.fold_in(streams_of[10], 71), 0)
    remote_tiles = centred(streams_of[2], (N_DOM, N_DOM, CAP, BLK, BLK), (8 * BLK) ** -0.5, 0.1875, ((0, 16),))
    remote_dst = with_ends(jax.random.randint(streams_of[3], (N_DOM, N_DOM, CAP), 0, 2 * NB), jax.random.fold_in(streams_of[3], 1), 0, (2 * NB) - 1).astype(jnp.int32)
    local_tiles = centred(streams_of[4], (LTILES, BLK, BLK), (8 * BLK) ** -0.5, 0.1875, ((0, 16),))
    local_src = with_ends(jax.random.randint(streams_of[5], (N_DOM, NL), 0, NB), jax.random.fold_in(streams_of[5], 1), 0, NB - 1).astype(jnp.int32)
    local_dst = with_ends(jax.random.randint(streams_of[6], (N_DOM, NL), 0, 2 * NB), jax.random.fold_in(streams_of[6], 1), 0, (2 * NB) - 1).astype(jnp.int32)
    weight = centred(streams_of[7], (F, F), F ** -0.5, 0.375, ((1, 2),))
    bias = centred(streams_of[8], (F,), 0.5, 3.0, ((0, 2),), jnp.float32)
    cotangent = centred(streams_of[9], (NODES, F), NODES ** -0.5, 0.046875, ((0, 16), (1, 2)))
    return {"history": history, "pull_list": pull_list, "remote_tiles": remote_tiles, "remote_dst": remote_dst, "local_tiles": local_tiles, "local_src": local_src, "local_dst": local_dst, "weight": weight, "bias": bias, "cotangent": cotangent}


def activate(value):
    return jax.nn.gelu(value, approximate=True)

def reference(history, pull_list, remote_tiles, remote_dst, local_tiles, local_src, local_dst, weight, bias, cotangent):
    blocks = history.reshape(N_DOM * NB, BLK, F)
    local_set = local_tiles.reshape(N_DOM, NL, BLK, BLK)
    row_ids = jnp.arange(2 * NB, dtype=jnp.int32)[:, None]

    def per_device(device):
        wanted = pull_list[device]
        owner_ids = jnp.arange(N_DOM, dtype=jnp.int32)[:, None]
        block_ids = (owner_ids * NB + jnp.clip(wanted, 0, NB - 1)).astype(jnp.int32)
        pulled = jnp.where((wanted >= 0)[:, :, None, None], blocks[block_ids], jnp.zeros((), blocks.dtype))
        products = jnp.einsum('ockj,ocjf->ockf', remote_tiles[device].astype(jnp.float32), pulled.astype(jnp.float32))
        pick_remote = (remote_dst[device].reshape(-1)[None, :] == row_ids).astype(jnp.float32)
        partial_value = jnp.dot(pick_remote, products.reshape(N_DOM * CAP, BLK * F), precision=lax.Precision.HIGHEST)
        sources = blocks[(device * NB + local_src[device]).astype(jnp.int32)]
        local_prod = jnp.einsum('kij,kjf->kif', local_set[device].astype(jnp.float32), sources.astype(jnp.float32))
        pick_local = (local_dst[device][None, :] == row_ids).astype(jnp.float32)
        return partial_value + jnp.dot(pick_local, local_prod.reshape(NL, BLK * F), precision=lax.Precision.HIGHEST)
    partials = lax.map(per_device, jnp.arange(N_DOM, dtype=jnp.int32))
    aggregate = partials[:, :NB] + jnp.roll(partials[:, NB:], 1, axis=0)
    aggregate = aggregate.reshape(NODES, F).astype(jnp.bfloat16)
    preact = jnp.dot(aggregate, weight, preferred_element_type=jnp.float32) + bias
    new_rows, backward_fn = jax.vjp(activate, preact)
    grad_pre = backward_fn(cotangent.astype(jnp.float32))[0].astype(jnp.bfloat16)
    grad_weight = lax.dot_general(aggregate, grad_pre, (((0,), (0,)), ((), ())), preferred_element_type=jnp.float32)
    grad_bias = lax.optimization_barrier(jnp.sum(grad_pre.astype(jnp.float32), axis=0))
    return (new_rows.astype(jnp.bfloat16), grad_weight, grad_bias)
```

```python
import functools

import jax
import jax.numpy as jnp
from jax import lax
from jax.experimental import pallas as pl
from jax.experimental.pallas import tpu as pltpu
from jax.sharding import PartitionSpec as P

PEERS = 4
VMEM = pl.BlockSpec(memory_space=pltpu.VMEM)
SMEM = pl.BlockSpec(memory_space=pltpu.SMEM)
PARAMS = pltpu.CompilerParams(vmem_limit_bytes=48 * 1024 * 1024)


def partner(block, bits):
    count = lax.axis_size("dom")
    return lax.ppermute(block, "dom", [(i, i ^ bits) for i in range(count)])


def passed_along(block, axis, distance):
    count = lax.axis_size(axis)
    return lax.ppermute(block, axis, [((i - distance) % count, i) for i in range(count)])


def local_kernel(count, src_ref, dst_ref, tiles_ref, blocks_ref, acc_ref):
    acc_ref[...] = jnp.zeros_like(acc_ref)

    def body(k, carry):
        product = jnp.dot(
            tiles_ref[k], blocks_ref[src_ref[k]], preferred_element_type=jnp.float32
        )
        dst = dst_ref[k]
        acc_ref[dst] = acc_ref[dst] + product
        return carry

    lax.fori_loop(0, count, body, 0, unroll=8)


def local_sum(src, dst, tiles, blocks, row_count):
    count, size, _ = tiles.shape
    return pl.pallas_call(
        functools.partial(local_kernel, count),
        out_shape=jax.ShapeDtypeStruct((row_count, size, blocks.shape[-1]), jnp.float32),
        in_specs=[SMEM, SMEM, VMEM, VMEM],
        out_specs=VMEM,
        compiler_params=PARAMS,
    )(src, dst, tiles, blocks)


def select_kernel(members, cap, me_ref, *refs):
    asked, held, out = refs[: PEERS - 1], refs[PEERS - 1 : -(PEERS - 1)], refs[-(PEERS - 1) :]
    for at, member in enumerate(members):
        owner = me_ref[0] ^ (member * PEERS)
        for j in range(PEERS - 1):
            for c in range(cap):
                wanted = jnp.maximum(asked[j][owner * cap + c], 0)
                out[j][at * cap + c] = held[at][wanted]


def select_blocks(me, asked, members, held, cap):
    size = held[0].shape[1:]
    shape = jax.ShapeDtypeStruct((len(members) * cap, *size), held[0].dtype)
    return pl.pallas_call(
        functools.partial(select_kernel, members, cap),
        out_shape=[shape] * (PEERS - 1),
        in_specs=[SMEM] * PEERS + [VMEM] * len(members),
        out_specs=[VMEM] * (PEERS - 1),
        compiler_params=PARAMS,
    )(me, *asked, *held)


def remote_kernel(members, cap, last, me_ref, wanted_ref, dst_ref, tiles_ref, acc_in, *refs):
    held = refs[: len(members)]
    pulled = refs[len(members) : len(members) + PEERS - 1]
    outs = refs[len(members) + PEERS - 1 :]
    acc = outs[0] if not last else outs[-1]
    acc[...] = acc_in[...]
    for at, member in enumerate(members):
        for j in range(PEERS):
            owner = me_ref[0] ^ (member * PEERS + j)
            for c in range(cap):
                slot = owner * cap + c
                wanted = wanted_ref[slot]
                if j == 0:
                    block = held[at][jnp.maximum(wanted, 0)]
                else:
                    block = pulled[j - 1][at * cap + c]
                block = jnp.where(wanted >= 0, block, jnp.zeros_like(block))
                product = jnp.dot(tiles_ref[slot], block, preferred_element_type=jnp.float32)
                dst = dst_ref[slot]
                acc[dst] = acc[dst] + product
    if last:
        own_ref, next_ref = outs[:2]
        half = own_ref.shape[0]
        own_ref[...] = acc[:half]
        next_ref[...] = acc[half:].astype(next_ref.dtype)


def remote_sum(me, wanted, dst, tiles, acc, members, held, pulled, cap, last):
    row_count, size, width = acc.shape
    shape = (row_count // 2, size, width)
    if last:
        out_shape = [
            jax.ShapeDtypeStruct(shape, jnp.float32),
            jax.ShapeDtypeStruct(shape, jnp.bfloat16),
        ]
        scratch = [pltpu.VMEM(acc.shape, jnp.float32)]
    else:
        out_shape = [jax.ShapeDtypeStruct(acc.shape, jnp.float32)]
        scratch = []
    return pl.pallas_call(
        functools.partial(remote_kernel, members, cap, last),
        out_shape=out_shape,
        in_specs=[SMEM] * 3 + [VMEM] * (2 + len(held) + len(pulled)),
        out_specs=[VMEM] * len(out_shape),
        scratch_shapes=scratch,
        compiler_params=PARAMS,
    )(me, wanted, dst, tiles, acc, *held, *pulled)


def activate(value):
    return jax.nn.gelu(value, approximate=True)


def per_device(
    history,
    pull_list,
    remote_tiles,
    remote_dst,
    local_tiles,
    local_src,
    local_dst,
    weight,
    bias,
    cotangent,
):
    count = lax.axis_size("dom")
    columns = count // PEERS
    cap = pull_list.shape[2]
    half_width = history.shape[1]
    block_size = local_tiles.shape[1]
    own_blocks = history.shape[0] // block_size
    row_count = 2 * own_blocks
    blocks = history.reshape(own_blocks, block_size, half_width)
    me = lax.axis_index("dom").astype(jnp.int32).reshape(1)
    wanted = pull_list.reshape(-1)
    targets = remote_dst.reshape(-1)
    tiles = remote_tiles.reshape(-1, block_size, block_size)

    held = {0: blocks}
    for member in sorted(range(1, columns), key=lambda k: (bin(k).count("1"), -k)):
        low = member & -member
        held[member] = partner(held[member ^ low], low * PEERS)
    asked = [partner(wanted, j) for j in range(1, PEERS)]

    acc = local_sum(local_src.reshape(-1), local_dst.reshape(-1), local_tiles, blocks, row_count)

    first, last = list(range(columns - 1)), [columns - 1]
    for members in (first, last):
        mine = [held[k] for k in members]
        picked = select_blocks(me, asked, members, mine, cap)
        pulled = [partner(picked[j - 1], j) for j in range(1, PEERS)]
        outs = remote_sum(
            me, wanted, targets, tiles, acc, members, mine, pulled, cap, members is last
        )
        acc = outs[0]
    own, following = outs

    incoming = passed_along(following, "dom", 1)
    aggregate = (
        (own + incoming.astype(jnp.float32))
        .reshape(own_blocks * block_size, half_width)
        .astype(jnp.bfloat16)
    )
    aggregate_full = lax.all_gather(aggregate, "feat", axis=1, tiled=True)
    preact = jnp.dot(aggregate_full, weight, preferred_element_type=jnp.float32) + bias
    new_rows, backward_fn = jax.vjp(activate, preact)
    grad_pre = backward_fn(cotangent.astype(jnp.float32))[0].astype(jnp.bfloat16)
    weight_term = lax.dot_general(
        aggregate_full, grad_pre, (((0,), (0,)), ((), ())), preferred_element_type=jnp.float32
    )
    bias_term = jnp.sum(grad_pre.astype(jnp.float32), axis=0)
    total = jnp.concatenate([weight_term, jnp.broadcast_to(bias_term, (8, half_width))])
    bits = 1
    while bits < count:
        total = total + partner(total, bits)
        bits *= 2
    grad_weight, grad_bias = total[: weight.shape[0]], total[weight.shape[0]]
    return (new_rows.astype(jnp.bfloat16), grad_weight, grad_bias)


def solution(mesh):
    placed = (
        P("dom", "feat"),
        P("dom", None, None),
        P("dom", None, None, None, None),
        P("dom", None, None),
        P("dom", None, None),
        P("dom", None),
        P("dom", None),
        P(None, "feat"),
        P("feat"),
        P("dom", "feat"),
    )
    return jax.shard_map(
        per_device,
        mesh=mesh,
        in_specs=placed,
        out_specs=(P("dom", "feat"), P(None, "feat"), P("feat")),
        check_vma=False,
    )
```

```python
import functools

import jax
import jax.numpy as jnp
from jax import lax
from jax.experimental import pallas as pl
from jax.experimental.pallas import tpu as pltpu
from jax.sharding import PartitionSpec as P

PEERS = 4
VMEM = pl.BlockSpec(memory_space=pltpu.VMEM)
SMEM = pl.BlockSpec(memory_space=pltpu.SMEM)
PARAMS = pltpu.CompilerParams(vmem_limit_bytes=48 * 1024 * 1024)


def partner(block, bits):
    count = lax.axis_size("dom")
    return lax.ppermute(block, "dom", [(i, i ^ bits) for i in range(count)])


def passed_along(block, axis, distance):
    count = lax.axis_size(axis)
    return lax.ppermute(block, axis, [((i - distance) % count, i) for i in range(count)])


def select_kernel(members, cap, me_ref, *refs):
    asked, held, out = refs[: PEERS - 1], refs[PEERS - 1 : -(PEERS - 1)], refs[-(PEERS - 1) :]
    for at, member in enumerate(members):
        owner = me_ref[0] ^ (member * PEERS)
        for j in range(PEERS - 1):
            for c in range(cap):
                wanted = jnp.maximum(asked[j][c, owner], 0)
                out[j][at * cap + c] = held[at][wanted]


def select_blocks(me, asked, members, held, cap):
    size = held[0].shape[1:]
    shape = jax.ShapeDtypeStruct((len(members) * cap, *size), held[0].dtype)
    return pl.pallas_call(
        functools.partial(select_kernel, members, cap),
        out_shape=[shape] * (PEERS - 1),
        in_specs=[SMEM] * PEERS + [VMEM] * len(members),
        out_specs=[VMEM] * (PEERS - 1),
        compiler_params=PARAMS,
    )(me, *asked, *held)


def begin_kernel(count, src_ref, dst_ref, tiles_ref, blocks_ref, acc):
    acc[...] = jnp.zeros_like(acc)

    def body(k, carry):
        product = jnp.dot(
            tiles_ref[k], blocks_ref[src_ref[0, k]], preferred_element_type=jnp.float32
        )
        dst = dst_ref[0, k]
        acc[dst] = acc[dst] + product
        return carry

    lax.fori_loop(0, count, body, 0, unroll=8)


def begin_sum(src, dst, tiles, blocks, row_count):
    count, size, _ = tiles.shape
    return pl.pallas_call(
        functools.partial(begin_kernel, count),
        out_shape=[jax.ShapeDtypeStruct((row_count, size, blocks.shape[-1]), jnp.float32)],
        in_specs=[SMEM, SMEM, VMEM, VMEM],
        out_specs=[VMEM],
        compiler_params=PARAMS,
    )(src, dst, tiles, blocks)


def sum_kernel(members, cap, last, *refs):
    refs = list(refs)
    me_ref, wanted_ref, dst_ref, tiles_ref = refs[:4]
    del refs[:4]
    held = [refs.pop(0) for _ in members]
    pulled = [refs.pop(0) for _ in range(PEERS - 1)]
    acc = refs[-1]
    acc[...] = refs[0][...]
    for at, member in enumerate(members):
        for j in range(PEERS):
            owner = me_ref[0] ^ (member * PEERS + j)
            for c in range(cap):
                wanted = wanted_ref[c, owner]
                if j == 0:
                    block = held[at][jnp.maximum(wanted, 0)]
                else:
                    block = pulled[j - 1][at * cap + c]
                block = jnp.where(wanted >= 0, block, jnp.zeros_like(block))
                product = jnp.dot(
                    tiles_ref[owner * cap + c], block, preferred_element_type=jnp.float32
                )
                dst = dst_ref[c, owner]
                acc[dst] = acc[dst] + product
    if last:
        own_ref, next_ref = refs[1:3]
        half = own_ref.shape[0]
        own_ref[...] = acc[:half]
        next_ref[...] = acc[half:].astype(next_ref.dtype)


def tile_sum(shared, members, held, pulled, cap, row_count, acc, last=False):
    size, width = held[0].shape[1:]
    full = (row_count, size, width)
    half = (row_count // 2, size, width)
    scratch = []
    out_shape = [jax.ShapeDtypeStruct(full, jnp.float32)]
    if last:
        out_shape = [
            jax.ShapeDtypeStruct(half, jnp.float32),
            jax.ShapeDtypeStruct(half, jnp.bfloat16),
        ]
        scratch = [pltpu.VMEM(full, jnp.float32)]
    return pl.pallas_call(
        functools.partial(sum_kernel, members, cap, last),
        out_shape=out_shape,
        in_specs=[SMEM] * 3 + [VMEM] * (2 + len(held) + len(pulled)),
        out_specs=[VMEM] * len(out_shape),
        scratch_shapes=scratch,
        compiler_params=PARAMS,
    )(*shared, *held, *pulled, acc)


def activate(value):
    return jax.nn.gelu(value, approximate=True)


def rounded(value):
    return lax.reduce_precision(value, 8, 7)


def finish_kernel(weight_refs, bias_ref, weight_out, bias_out):
    at = 0
    for mine, got in weight_refs:
        depth = mine.shape[0]
        weight_out[at : at + depth] = mine[...] + got[:depth].astype(jnp.float32)
        at += depth
    got = weight_refs[0][1]
    depth = weight_refs[0][0].shape[0]
    rows = got[depth:].astype(jnp.float32)
    bias_out[...] = bias_ref[...] + (rows[:1] + rows[8:9])


def finish(parts, bias_term):
    depth = sum(mine.shape[0] for mine, _ in parts)
    width = bias_term.shape[1]
    count = len(parts)

    def kernel(*refs):
        pairs = [(refs[2 * i], refs[2 * i + 1]) for i in range(count)]
        finish_kernel(pairs, refs[2 * count], refs[2 * count + 1], refs[2 * count + 2])

    return pl.pallas_call(
        kernel,
        out_shape=[
            jax.ShapeDtypeStruct((depth, width), jnp.float32),
            jax.ShapeDtypeStruct((1, width), jnp.float32),
        ],
        in_specs=[VMEM] * (2 * count + 1),
        out_specs=[VMEM] * 2,
        compiler_params=PARAMS,
    )(*[array for pair in parts for array in pair], bias_term)


def summed(weight_term, bias_term, count):
    depth, width = weight_term.shape
    bias_term = bias_term[None]
    got, bits = None, 1
    while bits < count:
        if got is not None:
            bias_term = bias_term + (got[depth : depth + 1] + got[depth + 8 : depth + 9])
            weight_term = weight_term + got[:depth]
        weight_term = rounded(weight_term)
        high = rounded(bias_term)
        low = rounded(bias_term - high)
        bias_term = high + low
        rows = [jnp.broadcast_to(row, (8, width)) for row in (high, low)]
        raw = partner(jnp.concatenate([weight_term, *rows]).astype(jnp.bfloat16), bits)
        got = raw.astype(jnp.float32)
        bits *= 2
    grad_weight, grad_bias = finish([(weight_term, raw)], bias_term)
    return grad_weight, grad_bias[0]


def per_device(
    history,
    pull_list,
    remote_tiles,
    remote_dst,
    local_tiles,
    local_src,
    local_dst,
    weight,
    bias,
    cotangent,
):
    count = lax.axis_size("dom")
    columns = count // PEERS
    cap = pull_list.shape[2]
    half_width = history.shape[1]
    block_size = local_tiles.shape[1]
    own_blocks = history.shape[0] // block_size
    row_count = 2 * own_blocks
    blocks = history.reshape(own_blocks, block_size, half_width)
    me = lax.axis_index("dom").astype(jnp.int32).reshape(1)
    wanted = pull_list[0].T
    tiles = remote_tiles.reshape(-1, block_size, block_size)
    shared = (me, wanted, remote_dst[0].T, tiles)

    def exchange(members, held):
        picked = select_blocks(me, asked, members, held, cap)
        return picked, [partner(picked[j - 1], j) for j in range(1, PEERS)]

    held = {0: blocks}
    for member in range(columns // 2, 0, -1):
        if member & (member - 1) == 0:
            held[member] = partner(blocks, member * PEERS)
    asked = [partner(wanted, j) for j in range(1, PEERS)]
    (acc,) = begin_sum(local_src, local_dst, local_tiles, blocks, row_count)
    for member in range(1, columns):
        if member not in held:
            low = member & -member
            source, acc, *asked = lax.optimization_barrier((held[member ^ low], acc, *asked))
            held[member] = partner(source, low * PEERS)

    first, last = list(range(columns - 1)), columns - 1
    held_first = [held[k] for k in first]
    picked, pulled_first = exchange(first, held_first)
    picked, pulled_last = exchange([last], [held[last]])
    (acc,) = tile_sum(shared, first, held_first, pulled_first, cap, row_count, acc=acc)
    outs = tile_sum(
        shared, [last], [held[last]], pulled_last, cap, row_count, acc=acc, last=True
    )
    own, following = outs

    incoming = passed_along(following, "dom", 1)
    aggregate = (
        (own + incoming.astype(jnp.float32))
        .reshape(own_blocks * block_size, half_width)
        .astype(jnp.bfloat16)
    )
    aggregate_full = lax.all_gather(aggregate, "feat", axis=1, tiled=True)
    preact = jnp.dot(aggregate_full, weight, preferred_element_type=jnp.float32) + bias
    new_rows, backward_fn = jax.vjp(activate, preact)
    grad_pre = backward_fn(cotangent.astype(jnp.float32))[0].astype(jnp.bfloat16)
    weight_term = lax.dot_general(
        aggregate_full, grad_pre, (((0,), (0,)), ((), ())), preferred_element_type=jnp.float32
    )
    bias_term = jnp.sum(grad_pre.astype(jnp.float32), axis=0)
    grad_weight, grad_bias = summed(weight_term, bias_term, count)
    return (new_rows.astype(jnp.bfloat16), grad_weight, grad_bias)


def solution(mesh):
    placed = (
        P("dom", "feat"),
        P("dom", None, None),
        P("dom", None, None, None, None),
        P("dom", None, None),
        P("dom", None, None),
        P("dom", None),
        P("dom", None),
        P(None, "feat"),
        P("feat"),
        P("dom", "feat"),
    )
    return jax.shard_map(
        per_device,
        mesh=mesh,
        in_specs=placed,
        out_specs=(P("dom", "feat"), P(None, "feat"), P("feat")),
        check_vma=False,
    )
```

```python
import functools

import jax
import jax.numpy as jnp
from jax import lax
from jax.experimental import pallas as pl
from jax.experimental.pallas import tpu as pltpu
from jax.sharding import PartitionSpec as P

PEERS = 4
VMEM = pl.BlockSpec(memory_space=pltpu.VMEM)
HBM = pl.BlockSpec(memory_space=pltpu.HBM)
SMEM = pl.BlockSpec(memory_space=pltpu.SMEM)
SLABS = 2
PARAMS = pltpu.CompilerParams(vmem_limit_bytes=48 * 1024 * 1024)


def partner(block, bits):
    count = lax.axis_size("dom")
    return lax.ppermute(block, "dom", [(i, i ^ bits) for i in range(count)])


def passed_along(block, axis, distance):
    count = lax.axis_size(axis)
    return lax.ppermute(block, axis, [((i - distance) % count, i) for i in range(count)])


def select_kernel(members, cap, me_ref, *refs):
    asked, held, out = refs[: PEERS - 1], refs[PEERS - 1 : -(PEERS - 1)], refs[-(PEERS - 1) :]
    for at, member in enumerate(members):
        owner = me_ref[0] ^ (member * PEERS)
        for j in range(PEERS - 1):
            for c in range(cap):
                wanted = jnp.maximum(asked[j][c, owner], 0)
                out[j][at * cap + c] = held[at][wanted]


def select_blocks(me, asked, members, held, cap):
    size = held[0].shape[1:]
    shape = jax.ShapeDtypeStruct((len(members) * cap, *size), held[0].dtype)
    return pl.pallas_call(
        functools.partial(select_kernel, members, cap),
        out_shape=[shape] * (PEERS - 1),
        in_specs=[SMEM] * PEERS + [VMEM] * len(members),
        out_specs=[VMEM] * (PEERS - 1),
        compiler_params=PARAMS,
    )(me, *asked, *held)


def begin_kernel(chunks, *refs):
    arrays, acc, held, sems = refs[:4], refs[4], refs[5:9], refs[9]
    src_ref, dst_ref, blocks_ref, tiles_ref = held
    per_chunk = tiles_ref.shape[0] // chunks
    whole = [pltpu.make_async_copy(arrays[i], held[i], sems.at[i]) for i in range(3)]
    parts = []
    for i in range(chunks):
        rows = pl.ds(i * per_chunk, per_chunk)
        parts.append(
            pltpu.make_async_copy(arrays[3].at[rows], tiles_ref.at[rows], sems.at[3 + i])
        )
    for copy in whole + parts:
        copy.start()
    acc[...] = jnp.zeros_like(acc)
    for copy in whole:
        copy.wait()
    for i in range(chunks):
        parts[i].wait()
        for k in range(i * per_chunk, (i + 1) * per_chunk):
            product = jnp.dot(
                tiles_ref[k], blocks_ref[src_ref[0, k]], preferred_element_type=jnp.float32
            )
            dst = dst_ref[0, k]
            acc[dst] = acc[dst] + product


def begin_sum(src, dst, tiles, blocks, row_count):
    count, size, _ = tiles.shape
    chunks = 8
    return pl.pallas_call(
        functools.partial(begin_kernel, chunks),
        out_shape=[jax.ShapeDtypeStruct((row_count, size, blocks.shape[-1]), jnp.float32)],
        in_specs=[HBM] * 4,
        out_specs=[VMEM],
        scratch_shapes=[
            pltpu.SMEM(src.shape, src.dtype),
            pltpu.SMEM(dst.shape, dst.dtype),
            pltpu.VMEM(blocks.shape, blocks.dtype),
            pltpu.VMEM(tiles.shape, tiles.dtype),
            pltpu.SemaphoreType.DMA((3 + chunks,)),
        ],
        compiler_params=PARAMS,
    )(*[pltpu.with_memory_space_constraint(x, pltpu.HBM) for x in (src, dst, blocks, tiles)])


def sum_kernel(sources, cap, last, me_ref, wanted_ref, dst_ref, tiles_ref, acc_in, *refs):
    acc = refs[-1]
    acc[...] = acc_in[...]
    for bits, at, start in sources:
        owner = me_ref[0] ^ bits
        for c in range(cap):
            wanted = wanted_ref[c, owner]
            block = refs[at][jnp.maximum(wanted, 0) if start is None else start + c]
            block = jnp.where(wanted >= 0, block, jnp.zeros_like(block))
            product = jnp.dot(
                tiles_ref[owner * cap + c], block, preferred_element_type=jnp.float32
            )
            dst = dst_ref[c, owner]
            acc[dst] = acc[dst] + product
    if last:
        own_ref, *next_refs = refs[-2 - SLABS : -1]
        at = own_ref.shape[0]
        own_ref[...] = acc[:at]
        for next_ref in next_refs:
            depth = next_ref.shape[0]
            next_ref[...] = acc[at : at + depth].astype(next_ref.dtype)
            at += depth


def tile_sum(shared, acc, sources, cap, last=False):
    row_count, size, width = acc.shape
    half = (row_count // 2, size, width)
    part = (row_count // 2 // SLABS, size, width)
    arrays, places = [], []
    for bits, array, start in sources:
        known = [i for i, other in enumerate(arrays) if other is array]
        if not known:
            known = [len(arrays)]
            arrays.append(array)
        places.append((bits, known[0], start))
    scratch = []
    out_shape = [jax.ShapeDtypeStruct(acc.shape, jnp.float32)]
    if last:
        out_shape = [jax.ShapeDtypeStruct(half, jnp.float32)]
        out_shape += [jax.ShapeDtypeStruct(part, jnp.bfloat16)] * SLABS
        scratch = [pltpu.VMEM(acc.shape, jnp.float32)]
    return pl.pallas_call(
        functools.partial(sum_kernel, places, cap, last),
        out_shape=out_shape,
        in_specs=[SMEM] * 3 + [VMEM] * (2 + len(arrays)),
        out_specs=[VMEM] * len(out_shape),
        scratch_shapes=scratch,
        compiler_params=PARAMS,
    )(*shared, acc, *arrays)


def dense_kernel(start, first, last, *refs):
    mine_ref, other_ref, weight_mine, weight_other, bias_ref, cot_ref = refs[:6]
    before = [] if first else refs[6:8]
    rows_ref, weight_out, bias_out = refs[6 + len(before) : 9 + len(before)]
    depth, width = mine_ref.shape
    step = min(depth, 256)
    terms = [jnp.zeros(weight_mine.shape, jnp.float32)] * 2 if first else [
        before[0][: weight_mine.shape[0]], before[0][weight_mine.shape[0] :]
    ]
    bias_sum = jnp.zeros((1, width), jnp.float32) if first else before[1][...]
    scale = 0.7978845608028654
    cubic = 0.044715
    for at in range(0, depth, step):
        mine, other = mine_ref[at : at + step], other_ref[at : at + step]
        v = (
            jnp.dot(mine, weight_mine[...], preferred_element_type=jnp.float32)
            + jnp.dot(other, weight_other[...], preferred_element_type=jnp.float32)
            + bias_ref[...]
        )
        square = v * v
        bent = jnp.tanh(scale * v * (1.0 + cubic * square))
        half = 0.5 * (1.0 + bent)
        rows_ref[at : at + step] = (v * half).astype(rows_ref.dtype)
        slope = half + 0.5 * v * (1.0 - bent * bent) * scale * (1.0 + 3.0 * cubic * square)
        cot = cot_ref[start + at : start + at + step].astype(jnp.float32)
        grad = (cot * slope).astype(jnp.bfloat16)
        bias_sum = bias_sum + jnp.sum(grad.astype(jnp.float32), axis=0, keepdims=True)
        for i, part in enumerate((mine, other)):
            terms[i] = terms[i] + lax.dot_general(
                part, grad, (((0,), (0,)), ((), ())), preferred_element_type=jnp.float32
            )
    if last:
        sent = refs[9 + len(before)]
        at = 0
        for term in terms:
            sent[at : at + width] = term.astype(sent.dtype)
            weight_out[at : at + width] = term.astype(sent.dtype).astype(jnp.float32)
            at += width
        high = bias_sum.astype(sent.dtype).astype(jnp.float32)
        low = (bias_sum - high).astype(sent.dtype).astype(jnp.float32)
        bias_out[...] = high + low
        for row in (high, low):
            sent[at : at + 8] = jnp.broadcast_to(row, (8, width)).astype(sent.dtype)
            at += 8
    else:
        weight_out[: weight_mine.shape[0]] = terms[0]
        weight_out[weight_mine.shape[0] :] = terms[1]
        bias_out[...] = bias_sum


def dense(mine, other, weights, bias, cotangent, start, before, last):
    depth, width = mine.shape
    rows = 2 * width
    out_shape = [
        jax.ShapeDtypeStruct((depth, width), jnp.bfloat16),
        jax.ShapeDtypeStruct((rows, width), jnp.float32),
        jax.ShapeDtypeStruct((1, width), jnp.float32),
    ]
    if last:
        out_shape.append(jax.ShapeDtypeStruct((rows + 16, width), jnp.bfloat16))
    return pl.pallas_call(
        functools.partial(dense_kernel, start, not before, last),
        out_shape=out_shape,
        in_specs=[VMEM] * (6 + len(before)),
        out_specs=[VMEM] * len(out_shape),
        compiler_params=PARAMS,
    )(mine, other, *weights, bias, cotangent, *before)


def rounded(value):
    return lax.reduce_precision(value, 8, 7)


def finish_kernel(feat_ref, weight_ref, bias_ref, got_ref, weight_out, bias_out):
    depth = weight_ref.shape[0]
    half = depth // 2
    feat = feat_ref[0]
    for at, place in ((0, feat), (half, 1 - feat)):
        weight_out[pl.ds(pl.multiple_of(place * half, half), half)] = weight_ref[
            at : at + half
        ] + got_ref[at : at + half].astype(jnp.float32)
    rows = got_ref[depth:].astype(jnp.float32)
    bias_out[...] = bias_ref[...] + (rows[:1] + rows[8:9])


def summed(weight_term, bias_term, sent, count, feat):
    depth, width = weight_term.shape
    bits = 1
    while True:
        raw = partner(sent, bits)
        bits *= 2
        if bits >= count:
            break
        got = raw.astype(jnp.float32)
        weight_term = rounded(weight_term + got[:depth])
        bias_term = bias_term + (got[depth : depth + 1] + got[depth + 8 : depth + 9])
        high = rounded(bias_term)
        low = rounded(bias_term - high)
        bias_term = high + low
        rows = [jnp.broadcast_to(row, (8, width)) for row in (high, low)]
        sent = jnp.concatenate([weight_term, *rows]).astype(jnp.bfloat16)
    return pl.pallas_call(
        finish_kernel,
        out_shape=[
            jax.ShapeDtypeStruct((depth, width), jnp.float32),
            jax.ShapeDtypeStruct((1, width), jnp.float32),
        ],
        in_specs=[SMEM] + [VMEM] * 3,
        out_specs=[VMEM] * 2,
        compiler_params=PARAMS,
    )(feat, weight_term, bias_term, raw)


def per_device(
    history,
    pull_list,
    remote_tiles,
    remote_dst,
    local_tiles,
    local_src,
    local_dst,
    weight,
    bias,
    cotangent,
):
    count = lax.axis_size("dom")
    columns = count // PEERS
    cap = pull_list.shape[2]
    half_width = history.shape[1]
    block_size = local_tiles.shape[1]
    own_blocks = history.shape[0] // block_size
    row_count = 2 * own_blocks
    blocks = history.reshape(own_blocks, block_size, half_width)
    me = lax.axis_index("dom").astype(jnp.int32).reshape(1)
    wanted = pull_list[0].T
    tiles = remote_tiles.reshape(-1, block_size, block_size)
    shared = (me, wanted, remote_dst[0].T, tiles)

    def exchange(members, after, hold=None):
        arrays = [held[k] for k in members]
        if after:
            arrays[0], *_ = lax.optimization_barrier((arrays[0], *after))
        picked = list(select_blocks(me, asked, members, arrays, cap))
        for j in [3]:
            if len(members) == 1:
                picked[j - 1], _ = lax.optimization_barrier((picked[j - 1], hold))
        pulled = [partner(picked[j - 1], j) for j in range(1, PEERS)]
        sources = []
        for at, member in enumerate(members):
            sources.append((member * PEERS, held[member], None))
            for j in range(1, PEERS):
                sources.append((member * PEERS + j, pulled[j - 1], at * cap))
        return sources, pulled, picked

    held = {0: blocks}
    for member in range(columns // 2, 0, -1):
        if member & (member - 1) == 0:
            held[member] = partner(blocks, member * PEERS)
    asked = [partner(wanted, j) for j in range(1, PEERS)]
    (acc,) = begin_sum(local_src, local_dst, local_tiles, blocks, row_count)
    for member in range(1, columns):
        if member not in held:
            low = member & -member
            source, acc, *asked = lax.optimization_barrier((held[member ^ low], acc, *asked))
            held[member] = partner(source, low * PEERS)

    first, arrived, _ = exchange(list(range(columns - 1)), [])
    rest, *_ = exchange([columns - 1], [], arrived[1])
    (acc,) = tile_sum(shared, acc, first, cap)
    outs = tile_sum(shared, acc, rest, cap, last=True)
    own, *following = outs
    incoming = [passed_along(part, "dom", 1) for part in following]

    feat = lax.axis_index("feat").astype(jnp.int32).reshape(1)
    weights = [
        lax.dynamic_slice_in_dim(weight, place * half_width, half_width)
        for place in (feat[0], 1 - feat[0])
    ]
    depth = own_blocks // SLABS
    before, new_rows = [], []
    for at, part in enumerate(incoming):
        mine = (own[at * depth : (at + 1) * depth] + part.astype(jnp.float32)).astype(jnp.bfloat16)
        mine = mine.reshape(depth * block_size, half_width)
        other = passed_along(mine, "feat", 1)
        rows, *before = dense(
            mine,
            other,
            weights,
            bias[None],
            cotangent,
            at * depth * block_size,
            before,
            at == SLABS - 1,
        )
        new_rows.append(rows)
    grad_weight, grad_bias = summed(*before, count, feat)
    return (jnp.concatenate(new_rows), grad_weight, grad_bias[0])


def solution(mesh):
    placed = (
        P("dom", "feat"),
        P("dom", None, None),
        P("dom", None, None, None, None),
        P("dom", None, None),
        P("dom", None, None),
        P("dom", None),
        P("dom", None),
        P(None, "feat"),
        P("feat"),
        P("dom", "feat"),
    )
    return jax.shard_map(
        per_device,
        mesh=mesh,
        in_specs=placed,
        out_specs=(P("dom", "feat"), P(None, "feat"), P("feat")),
        check_vma=False,
    )
```

```python
import functools

import jax
import jax.numpy as jnp
from jax import lax
from jax.experimental import pallas as pl
from jax.experimental.pallas import tpu as pltpu
from jax.sharding import PartitionSpec as P

PEERS = 4
VMEM = pl.BlockSpec(memory_space=pltpu.VMEM)
HBM = pl.BlockSpec(memory_space=pltpu.HBM)
SMEM = pl.BlockSpec(memory_space=pltpu.SMEM)
SLABS = 2
PARAMS = pltpu.CompilerParams(vmem_limit_bytes=48 * 1024 * 1024)


def partner(block, bits):
    count = lax.axis_size("dom")
    return lax.ppermute(block, "dom", [(i, i ^ bits) for i in range(count)])


def passed_along(block, axis, distance):
    count = lax.axis_size(axis)
    return lax.ppermute(block, axis, [((i - distance) % count, i) for i in range(count)])


def select_kernel(members, cap, me_ref, *refs):
    asked, held, out = refs[: PEERS - 1], refs[PEERS - 1 : -(PEERS - 1)], refs[-(PEERS - 1) :]
    for at, member in enumerate(members):
        owner = me_ref[0] ^ (member * PEERS)
        for j in range(PEERS - 1):
            for c in range(cap):
                wanted = jnp.maximum(asked[j][c, owner], 0)
                out[j][at * cap + c] = held[at][wanted]


def select_blocks(me, asked, members, held, cap):
    size = held[0].shape[1:]
    shape = jax.ShapeDtypeStruct((len(members) * cap, *size), held[0].dtype)
    return pl.pallas_call(
        functools.partial(select_kernel, members, cap),
        out_shape=[shape] * (PEERS - 1),
        in_specs=[SMEM] * PEERS + [VMEM] * len(members),
        out_specs=[VMEM] * (PEERS - 1),
        compiler_params=PARAMS,
    )(me, *asked, *held)


def begin_kernel(chunks, *refs):
    arrays, acc, held, sems = refs[:4], refs[4], refs[5:9], refs[9]
    src_ref, dst_ref, blocks_ref, tiles_ref = held
    per_chunk = tiles_ref.shape[0] // chunks
    whole = [pltpu.make_async_copy(arrays[i], held[i], sems.at[i]) for i in range(3)]
    parts = []
    for i in range(chunks):
        rows = pl.ds(i * per_chunk, per_chunk)
        parts.append(
            pltpu.make_async_copy(arrays[3].at[rows], tiles_ref.at[rows], sems.at[3 + i])
        )
    for copy in whole + parts:
        copy.start()
    acc[...] = jnp.zeros_like(acc)
    for copy in whole:
        copy.wait()
    for i in range(chunks):
        parts[i].wait()
        for k in range(i * per_chunk, (i + 1) * per_chunk):
            product = jnp.dot(
                tiles_ref[k], blocks_ref[src_ref[0, k]], preferred_element_type=jnp.float32
            )
            dst = dst_ref[0, k]
            acc[dst] = acc[dst] + product


def begin_sum(src, dst, tiles, blocks, row_count):
    count, size, _ = tiles.shape
    chunks = 8
    return pl.pallas_call(
        functools.partial(begin_kernel, chunks),
        out_shape=[jax.ShapeDtypeStruct((row_count, size, blocks.shape[-1]), jnp.float32)],
        in_specs=[HBM] * 4,
        out_specs=[VMEM],
        scratch_shapes=[
            pltpu.SMEM(src.shape, src.dtype),
            pltpu.SMEM(dst.shape, dst.dtype),
            pltpu.VMEM(blocks.shape, blocks.dtype),
            pltpu.VMEM(tiles.shape, tiles.dtype),
            pltpu.SemaphoreType.DMA((3 + chunks,)),
        ],
        compiler_params=PARAMS,
    )(*[pltpu.with_memory_space_constraint(x, pltpu.HBM) for x in (src, dst, blocks, tiles)])


def sum_kernel(sources, cap, last, me_ref, wanted_ref, dst_ref, tiles_ref, acc_in, *refs):
    acc = refs[-1]
    acc[...] = acc_in[...]
    for bits, at, start in sources:
        owner = me_ref[0] ^ bits
        for c in range(cap):
            wanted = wanted_ref[c, owner]
            block = refs[at][jnp.maximum(wanted, 0) if start is None else start + c]
            block = jnp.where(wanted >= 0, block, jnp.zeros_like(block))
            product = jnp.dot(
                tiles_ref[owner * cap + c], block, preferred_element_type=jnp.float32
            )
            dst = dst_ref[c, owner]
            acc[dst] = acc[dst] + product
    if last:
        own_ref, *next_refs = refs[-2 - SLABS : -1]
        at = own_ref.shape[0]
        own_ref[...] = acc[:at]
        for next_ref in next_refs:
            depth = next_ref.shape[0]
            next_ref[...] = acc[at : at + depth].astype(next_ref.dtype)
            at += depth


def tile_sum(shared, acc, sources, cap, last=False):
    row_count, size, width = acc.shape
    half = (row_count // 2, size, width)
    part = (row_count // 2 // SLABS, size, width)
    arrays, places = [], []
    for bits, array, start in sources:
        known = [i for i, other in enumerate(arrays) if other is array]
        if not known:
            known = [len(arrays)]
            arrays.append(array)
        places.append((bits, known[0], start))
    scratch = []
    out_shape = [jax.ShapeDtypeStruct(acc.shape, jnp.float32)]
    if last:
        out_shape = [jax.ShapeDtypeStruct(half, jnp.float32)]
        out_shape += [jax.ShapeDtypeStruct(part, jnp.bfloat16)] * SLABS
        scratch = [pltpu.VMEM(acc.shape, jnp.float32)]
    return pl.pallas_call(
        functools.partial(sum_kernel, places, cap, last),
        out_shape=out_shape,
        in_specs=[SMEM] * 3 + [VMEM] * (2 + len(arrays)),
        out_specs=[VMEM] * len(out_shape),
        scratch_shapes=scratch,
        compiler_params=PARAMS,
    )(*shared, acc, *arrays)


def dense_kernel(start, first, last, *refs):
    mine_ref, other_ref, weight_mine, weight_other, bias_ref, cot_ref = refs[:6]
    before = [] if first else refs[6:8]
    rows_ref, weight_out, bias_out = refs[6 + len(before) : 9 + len(before)]
    depth, width = mine_ref.shape
    step = min(depth, 256)
    terms = [jnp.zeros(weight_mine.shape, jnp.float32)] * 2 if first else [
        before[0][: weight_mine.shape[0]], before[0][weight_mine.shape[0] :]
    ]
    bias_sum = jnp.zeros((1, width), jnp.float32) if first else before[1][...]
    scale = 0.7978845608028654
    cubic = 0.044715
    for at in range(0, depth, step):
        mine, other = mine_ref[at : at + step], other_ref[at : at + step]
        v = (
            jnp.dot(mine, weight_mine[...], preferred_element_type=jnp.float32)
            + jnp.dot(other, weight_other[...], preferred_element_type=jnp.float32)
            + bias_ref[...]
        )
        square = v * v
        bent = jnp.tanh(scale * v * (1.0 + cubic * square))
        half = 0.5 * (1.0 + bent)
        rows_ref[at : at + step] = (v * half).astype(rows_ref.dtype)
        slope = half + 0.5 * v * (1.0 - bent * bent) * scale * (1.0 + 3.0 * cubic * square)
        cot = cot_ref[start + at : start + at + step].astype(jnp.float32)
        grad = (cot * slope).astype(jnp.bfloat16)
        bias_sum = bias_sum + jnp.sum(grad.astype(jnp.float32), axis=0, keepdims=True)
        for i, part in enumerate((mine, other)):
            terms[i] = terms[i] + lax.dot_general(
                part, grad, (((0,), (0,)), ((), ())), preferred_element_type=jnp.float32
            )
    if last:
        sent = refs[9 + len(before)]
        at = 0
        for term in terms:
            sent[at : at + width] = term.astype(sent.dtype)
            weight_out[at : at + width] = term.astype(sent.dtype).astype(jnp.float32)
            at += width
        high = bias_sum.astype(sent.dtype).astype(jnp.float32)
        low = (bias_sum - high).astype(sent.dtype).astype(jnp.float32)
        bias_out[...] = high + low
        for row in (high, low):
            sent[at : at + 8] = jnp.broadcast_to(row, (8, width)).astype(sent.dtype)
            at += 8
    else:
        weight_out[: weight_mine.shape[0]] = terms[0]
        weight_out[weight_mine.shape[0] :] = terms[1]
        bias_out[...] = bias_sum


def dense(mine, other, weights, bias, cotangent, start, before, last):
    depth, width = mine.shape
    rows = 2 * width
    out_shape = [
        jax.ShapeDtypeStruct((depth, width), jnp.bfloat16),
        jax.ShapeDtypeStruct((rows, width), jnp.float32),
        jax.ShapeDtypeStruct((1, width), jnp.float32),
    ]
    if last:
        out_shape.append(jax.ShapeDtypeStruct((rows + 16, width), jnp.bfloat16))
    return pl.pallas_call(
        functools.partial(dense_kernel, start, not before, last),
        out_shape=out_shape,
        in_specs=[VMEM] * (6 + len(before)),
        out_specs=[VMEM] * len(out_shape),
        compiler_params=PARAMS,
    )(mine, other, *weights, bias, cotangent, *before)


def rounded(value):
    return lax.reduce_precision(value, 8, 7)


def finish_kernel(feat_ref, weight_ref, bias_ref, *refs):
    *got_refs, weight_out, bias_out = refs
    depth = weight_ref.shape[0]
    half = depth // 2
    feat = feat_ref[0]

    def total(mine, start, rows):
        got = [ref[start : start + rows].astype(jnp.float32) for ref in got_refs]
        mine = mine + got[0]
        return mine + (got[1] + got[2]) if len(got) > 1 else mine

    for at, place in ((0, feat), (half, 1 - feat)):
        weight_out[pl.ds(pl.multiple_of(place * half, half), half)] = total(
            weight_ref[at : at + half], at, half
        )
    rows = [ref[depth:].astype(jnp.float32) for ref in got_refs]
    rows = [part[:1] + part[8:9] for part in rows]
    bias = bias_ref[...] + rows[0]
    bias_out[...] = bias + (rows[1] + rows[2]) if len(rows) > 1 else bias


def summed(weight_term, bias_term, sent, count, feat):
    depth, width = weight_term.shape

    def taken(raw):
        got = raw.astype(jnp.float32)
        return got[:depth], got[depth : depth + 1] + got[depth + 8 : depth + 9]

    plan, bits = [], 1
    while bits < count:
        plan.append([bits * j for j in range(1, min(PEERS, count // bits))])
        bits *= PEERS
    for at, bits in enumerate(plan):
        raw = [partner(sent, k) for k in bits]
        if at == len(plan) - 1:
            break
        got = [taken(part) for part in raw]
        weight_term, bias_term = weight_term + got[0][0], bias_term + got[0][1]
        if len(got) > 1:
            weight_term = weight_term + (got[1][0] + got[2][0])
            bias_term = bias_term + (got[1][1] + got[2][1])
        weight_term = rounded(weight_term)
        high = rounded(bias_term)
        low = rounded(bias_term - high)
        bias_term = high + low
        rows = [jnp.broadcast_to(row, (8, width)) for row in (high, low)]
        sent = jnp.concatenate([weight_term, *rows]).astype(jnp.bfloat16)
    return pl.pallas_call(
        finish_kernel,
        out_shape=[
            jax.ShapeDtypeStruct((depth, width), jnp.float32),
            jax.ShapeDtypeStruct((1, width), jnp.float32),
        ],
        in_specs=[SMEM] + [VMEM] * (2 + len(raw)),
        out_specs=[VMEM] * 2,
        compiler_params=PARAMS,
    )(feat, weight_term, bias_term, *raw)


def per_device(
    history,
    pull_list,
    remote_tiles,
    remote_dst,
    local_tiles,
    local_src,
    local_dst,
    weight,
    bias,
    cotangent,
):
    count = lax.axis_size("dom")
    columns = count // PEERS
    cap = pull_list.shape[2]
    half_width = history.shape[1]
    block_size = local_tiles.shape[1]
    own_blocks = history.shape[0] // block_size
    row_count = 2 * own_blocks
    blocks = history.reshape(own_blocks, block_size, half_width)
    me = lax.axis_index("dom").astype(jnp.int32).reshape(1)
    wanted = pull_list[0].T
    tiles = remote_tiles.reshape(-1, block_size, block_size)
    shared = (me, wanted, remote_dst[0].T, tiles)

    def exchange(members, after, hold=None):
        arrays = [held[k] for k in members]
        if after:
            arrays[0], *_ = lax.optimization_barrier((arrays[0], *after))
        picked = list(select_blocks(me, asked, members, arrays, cap))
        for j in [3]:
            if len(members) == 1:
                picked[j - 1], _ = lax.optimization_barrier((picked[j - 1], hold))
        pulled = [partner(picked[j - 1], j) for j in range(1, PEERS)]
        sources = []
        for at, member in enumerate(members):
            sources.append((member * PEERS, held[member], None))
            for j in range(1, PEERS):
                sources.append((member * PEERS + j, pulled[j - 1], at * cap))
        return sources, pulled, picked

    held = {0: blocks}
    for member in range(columns // 2, 0, -1):
        if member & (member - 1) == 0:
            held[member] = partner(blocks, member * PEERS)
    asked = [partner(wanted, j) for j in range(1, PEERS)]
    (acc,) = begin_sum(local_src, local_dst, local_tiles, blocks, row_count)
    for member in range(1, columns):
        if member not in held:
            low = member & -member
            source, acc, *asked = lax.optimization_barrier((held[member ^ low], acc, *asked))
            held[member] = partner(source, low * PEERS)

    first, arrived, _ = exchange(list(range(columns - 1)), [])
    rest, *_ = exchange([columns - 1], [], arrived[1])
    (acc,) = tile_sum(shared, acc, first, cap)
    outs = tile_sum(shared, acc, rest, cap, last=True)
    own, *following = outs
    incoming = [passed_along(part, "dom", 1) for part in following]

    feat = lax.axis_index("feat").astype(jnp.int32).reshape(1)
    weights = [
        lax.dynamic_slice_in_dim(weight, place * half_width, half_width)
        for place in (feat[0], 1 - feat[0])
    ]
    depth = own_blocks // SLABS
    before, new_rows = [], []
    for at, part in enumerate(incoming):
        mine = (own[at * depth : (at + 1) * depth] + part.astype(jnp.float32)).astype(jnp.bfloat16)
        mine = mine.reshape(depth * block_size, half_width)
        other = passed_along(mine, "feat", 1)
        rows, *before = dense(
            mine,
            other,
            weights,
            bias[None],
            cotangent,
            at * depth * block_size,
            before,
            at == SLABS - 1,
        )
        new_rows.append(rows)
    grad_weight, grad_bias = summed(*before, count, feat)
    return (jnp.concatenate(new_rows), grad_weight, grad_bias[0])


def solution(mesh):
    placed = (
        P("dom", "feat"),
        P("dom", None, None),
        P("dom", None, None, None, None),
        P("dom", None, None),
        P("dom", None, None),
        P("dom", None),
        P("dom", None),
        P(None, "feat"),
        P("feat"),
        P("dom", "feat"),
    )
    return jax.shard_map(
        per_device,
        mesh=mesh,
        in_specs=placed,
        out_specs=(P("dom", "feat"), P(None, "feat"), P("feat")),
        check_vma=False,
    )
```

```python
import functools

import jax
import jax.numpy as jnp
from jax import lax
from jax.experimental import pallas as pl
from jax.experimental.pallas import tpu as pltpu
from jax.sharding import PartitionSpec as P

PEERS = 4
VMEM = pl.BlockSpec(memory_space=pltpu.VMEM)
HBM = pl.BlockSpec(memory_space=pltpu.HBM)
SMEM = pl.BlockSpec(memory_space=pltpu.SMEM)
SLABS = 2
PARAMS = pltpu.CompilerParams(vmem_limit_bytes=48 * 1024 * 1024)


def partner(block, bits):
    count = lax.axis_size("dom")
    return lax.ppermute(block, "dom", [(i, i ^ bits) for i in range(count)])


def passed_along(block, axis, distance):
    count = lax.axis_size(axis)
    return lax.ppermute(block, axis, [((i - distance) % count, i) for i in range(count)])


def select_kernel(members, cap, me_ref, *refs):
    asked, held, out = refs[: PEERS - 1], refs[PEERS - 1 : -(PEERS - 1)], refs[-(PEERS - 1) :]
    for at, member in enumerate(members):
        owner = me_ref[0] ^ (member * PEERS)
        for j in range(PEERS - 1):
            for c in range(cap):
                wanted = jnp.maximum(asked[j][c, owner], 0)
                out[j][at * cap + c] = held[at][wanted]


def select_blocks(me, asked, members, held, cap):
    size = held[0].shape[1:]
    shape = jax.ShapeDtypeStruct((len(members) * cap, *size), held[0].dtype)
    return pl.pallas_call(
        functools.partial(select_kernel, members, cap),
        out_shape=[shape] * (PEERS - 1),
        in_specs=[SMEM] * PEERS + [VMEM] * len(members),
        out_specs=[VMEM] * (PEERS - 1),
        compiler_params=PARAMS,
    )(me, *asked, *held)


def begin_kernel(chunks, *refs):
    arrays, acc, held, sems = refs[:4], refs[4], refs[5:9], refs[9]
    src_ref, dst_ref, blocks_ref, tiles_ref = held
    per_chunk = tiles_ref.shape[0] // chunks
    whole = [pltpu.make_async_copy(arrays[i], held[i], sems.at[i]) for i in range(3)]
    parts = []
    for i in range(chunks):
        rows = pl.ds(i * per_chunk, per_chunk)
        parts.append(
            pltpu.make_async_copy(arrays[3].at[rows], tiles_ref.at[rows], sems.at[3 + i])
        )
    for copy in whole + parts:
        copy.start()
    acc[...] = jnp.zeros_like(acc)
    for copy in whole:
        copy.wait()
    for i in range(chunks):
        parts[i].wait()
        for k in range(i * per_chunk, (i + 1) * per_chunk):
            product = jnp.dot(
                tiles_ref[k], blocks_ref[src_ref[0, k]], preferred_element_type=jnp.float32
            )
            dst = dst_ref[0, k]
            acc[dst] = acc[dst] + product


def begin_sum(src, dst, tiles, blocks, row_count):
    count, size, _ = tiles.shape
    chunks = 8
    return pl.pallas_call(
        functools.partial(begin_kernel, chunks),
        out_shape=[jax.ShapeDtypeStruct((row_count, size, blocks.shape[-1]), jnp.float32)],
        in_specs=[HBM] * 4,
        out_specs=[VMEM],
        scratch_shapes=[
            pltpu.SMEM(src.shape, src.dtype),
            pltpu.SMEM(dst.shape, dst.dtype),
            pltpu.VMEM(blocks.shape, blocks.dtype),
            pltpu.VMEM(tiles.shape, tiles.dtype),
            pltpu.SemaphoreType.DMA((3 + chunks,)),
        ],
        compiler_params=PARAMS,
    )(*[pltpu.with_memory_space_constraint(x, pltpu.HBM) for x in (src, dst, blocks, tiles)])


def sum_kernel(sources, cap, last, me_ref, wanted_ref, dst_ref, tiles_ref, acc_in, *refs):
    acc = refs[-1]
    acc[...] = acc_in[...]
    for bits, at, start in sources:
        owner = me_ref[0] ^ bits
        for c in range(cap):
            wanted = wanted_ref[c, owner]
            block = refs[at][jnp.maximum(wanted, 0) if start is None else start + c]
            block = jnp.where(wanted >= 0, block, jnp.zeros_like(block))
            product = jnp.dot(
                tiles_ref[owner * cap + c], block, preferred_element_type=jnp.float32
            )
            dst = dst_ref[c, owner]
            acc[dst] = acc[dst] + product
    if last:
        own_ref, *next_refs = refs[-2 - SLABS : -1]
        at = own_ref.shape[0]
        own_ref[...] = acc[:at]
        for next_ref in next_refs:
            depth = next_ref.shape[0]
            next_ref[...] = acc[at : at + depth].astype(next_ref.dtype)
            at += depth


def tile_sum(shared, acc, sources, cap, last=False):
    row_count, size, width = acc.shape
    half = (row_count // 2, size, width)
    part = (row_count // 2 // SLABS, size, width)
    arrays, places = [], []
    for bits, array, start in sources:
        known = [i for i, other in enumerate(arrays) if other is array]
        if not known:
            known = [len(arrays)]
            arrays.append(array)
        places.append((bits, known[0], start))
    scratch = []
    out_shape = [jax.ShapeDtypeStruct(acc.shape, jnp.float32)]
    if last:
        out_shape = [jax.ShapeDtypeStruct(half, jnp.float32)]
        out_shape += [jax.ShapeDtypeStruct(part, jnp.bfloat16)] * SLABS
        scratch = [pltpu.VMEM(acc.shape, jnp.float32)]
    return pl.pallas_call(
        functools.partial(sum_kernel, places, cap, last),
        out_shape=out_shape,
        in_specs=[SMEM] * 3 + [VMEM] * (2 + len(arrays)),
        out_specs=[VMEM] * len(out_shape),
        scratch_shapes=scratch,
        compiler_params=PARAMS,
    )(*shared, acc, *arrays)


def dense_kernel(start, first, last, *refs):
    mine_ref, other_ref, weight_mine, weight_other, bias_ref, cot_ref = refs[:6]
    before = [] if first else refs[6:8]
    rows_ref, weight_out, bias_out = refs[6 + len(before) : 9 + len(before)]
    depth, width = mine_ref.shape
    step = min(depth, 256)
    terms = [jnp.zeros(weight_mine.shape, jnp.float32)] * 2 if first else [
        before[0][: weight_mine.shape[0]], before[0][weight_mine.shape[0] :]
    ]
    bias_sum = jnp.zeros((1, width), jnp.float32) if first else before[1][...]
    scale = 0.7978845608028654
    cubic = 0.044715
    for at in range(0, depth, step):
        mine, other = mine_ref[at : at + step], other_ref[at : at + step]
        v = (
            jnp.dot(mine, weight_mine[...], preferred_element_type=jnp.float32)
            + jnp.dot(other, weight_other[...], preferred_element_type=jnp.float32)
            + bias_ref[...]
        )
        square = v * v
        bent = jnp.tanh(scale * v * (1.0 + cubic * square))
        half = 0.5 * (1.0 + bent)
        rows_ref[at : at + step] = (v * half).astype(rows_ref.dtype)
        slope = half + 0.5 * v * (1.0 - bent * bent) * scale * (1.0 + 3.0 * cubic * square)
        cot = cot_ref[start + at : start + at + step].astype(jnp.float32)
        grad = (cot * slope).astype(jnp.bfloat16)
        bias_sum = bias_sum + jnp.sum(grad.astype(jnp.float32), axis=0, keepdims=True)
        for i, part in enumerate((mine, other)):
            terms[i] = terms[i] + lax.dot_general(
                part, grad, (((0,), (0,)), ((), ())), preferred_element_type=jnp.float32
            )
    if last:
        sent = refs[9 + len(before)]
        at = 0
        for term in terms:
            sent[at : at + width] = term.astype(sent.dtype)
            weight_out[at : at + width] = term.astype(sent.dtype).astype(jnp.float32)
            at += width
        high = bias_sum.astype(sent.dtype).astype(jnp.float32)
        low = (bias_sum - high).astype(sent.dtype).astype(jnp.float32)
        bias_out[...] = high + low
        for row in (high, low):
            sent[at : at + 8] = jnp.broadcast_to(row, (8, width)).astype(sent.dtype)
            at += 8
    else:
        weight_out[: weight_mine.shape[0]] = terms[0]
        weight_out[weight_mine.shape[0] :] = terms[1]
        bias_out[...] = bias_sum


def dense(mine, other, weights, bias, cotangent, start, before, last):
    depth, width = mine.shape
    rows = 2 * width
    out_shape = [
        jax.ShapeDtypeStruct((depth, width), jnp.bfloat16),
        jax.ShapeDtypeStruct((rows, width), jnp.float32),
        jax.ShapeDtypeStruct((1, width), jnp.float32),
    ]
    if last:
        out_shape.append(jax.ShapeDtypeStruct((rows + 16, width), jnp.bfloat16))
    return pl.pallas_call(
        functools.partial(dense_kernel, start, not before, last),
        out_shape=out_shape,
        in_specs=[VMEM] * (6 + len(before)),
        out_specs=[VMEM] * len(out_shape),
        compiler_params=PARAMS,
    )(mine, other, *weights, bias, cotangent, *before)


def rounded(value):
    return lax.reduce_precision(value, 8, 7)


def finish_kernel(feat_ref, weight_ref, bias_ref, *refs):
    *got_refs, weight_out, bias_out = refs
    depth = weight_ref.shape[0]
    half = depth // 2
    feat = feat_ref[0]

    def total(mine, start, rows):
        got = [ref[start : start + rows].astype(jnp.float32) for ref in got_refs]
        mine = mine + got[0]
        return mine + (got[1] + got[2]) if len(got) > 1 else mine

    for at, place in ((0, feat), (half, 1 - feat)):
        weight_out[pl.ds(pl.multiple_of(place * half, half), half)] = total(
            weight_ref[at : at + half], at, half
        )
    rows = [ref[depth:].astype(jnp.float32) for ref in got_refs]
    rows = [part[:1] + part[8:9] for part in rows]
    bias = bias_ref[...] + rows[0]
    bias_out[...] = bias + (rows[1] + rows[2]) if len(rows) > 1 else bias


def summed(weight_term, bias_term, sent, count, feat):
    depth, width = weight_term.shape

    def taken(raw):
        got = raw.astype(jnp.float32)
        return got[:depth], got[depth : depth + 1] + got[depth + 8 : depth + 9]

    plan, bits = [], 1
    while bits < count:
        plan.append([bits * j for j in range(1, min(PEERS, count // bits))])
        bits *= PEERS
    for at, bits in enumerate(plan):
        raw = [partner(sent, k) for k in bits]
        if at == len(plan) - 1:
            break
        got = [taken(part) for part in raw]
        weight_term, bias_term = weight_term + got[0][0], bias_term + got[0][1]
        if len(got) > 1:
            weight_term = weight_term + (got[1][0] + got[2][0])
            bias_term = bias_term + (got[1][1] + got[2][1])
        weight_term = rounded(weight_term)
        high = rounded(bias_term)
        low = rounded(bias_term - high)
        bias_term = high + low
        rows = [jnp.broadcast_to(row, (8, width)) for row in (high, low)]
        sent = jnp.concatenate([weight_term, *rows]).astype(jnp.bfloat16)
    return pl.pallas_call(
        finish_kernel,
        out_shape=[
            jax.ShapeDtypeStruct((depth, width), jnp.float32),
            jax.ShapeDtypeStruct((1, width), jnp.float32),
        ],
        in_specs=[SMEM] + [VMEM] * (2 + len(raw)),
        out_specs=[VMEM] * 2,
        compiler_params=PARAMS,
    )(feat, weight_term, bias_term, *raw)


def per_device(
    history,
    pull_list,
    remote_tiles,
    remote_dst,
    local_tiles,
    local_src,
    local_dst,
    weight,
    bias,
    cotangent,
):
    count = lax.axis_size("dom")
    columns = count // PEERS
    cap = pull_list.shape[2]
    half_width = history.shape[1]
    block_size = local_tiles.shape[1]
    own_blocks = history.shape[0] // block_size
    row_count = 2 * own_blocks
    blocks = history.reshape(own_blocks, block_size, half_width)
    me = lax.axis_index("dom").astype(jnp.int32).reshape(1)
    wanted = pull_list[0].T
    tiles = remote_tiles.reshape(-1, block_size, block_size)
    shared = (me, wanted, remote_dst[0].T, tiles)

    def exchange(members, after, hold=None):
        arrays = [held[k] for k in members]
        if after:
            arrays[0], *_ = lax.optimization_barrier((arrays[0], *after))
        picked = list(select_blocks(me, asked, members, arrays, cap))
        for j in [3]:
            if len(members) == 1:
                picked[j - 1], _ = lax.optimization_barrier((picked[j - 1], hold))
        pulled = [partner(picked[j - 1], j) for j in range(1, PEERS)]
        sources = []
        for at, member in enumerate(members):
            sources.append((member * PEERS, held[member], None))
            for j in range(1, PEERS):
                sources.append((member * PEERS + j, pulled[j - 1], at * cap))
        return sources, pulled, picked

    held = {0: blocks}
    for member in range(columns // 2, 0, -1):
        if member & (member - 1) == 0:
            held[member] = partner(blocks, member * PEERS)
    asked = [partner(wanted, j) for j in range(1, PEERS)]
    (acc,) = begin_sum(local_src, local_dst, local_tiles, blocks, row_count)
    for member in range(1, columns):
        if member not in held:
            low = member & -member
            source, acc, *asked = lax.optimization_barrier((held[member ^ low], acc, *asked))
            held[member] = partner(source, low * PEERS)

    first, arrived, _ = exchange(list(range(columns - 1)), [])
    rest, *_ = exchange([columns - 1], [], arrived[1])
    (acc,) = tile_sum(shared, acc, first, cap)
    outs = tile_sum(shared, acc, rest, cap, last=True)
    own, *following = outs
    incoming = [passed_along(part, "dom", 1) for part in following]

    feat = lax.axis_index("feat").astype(jnp.int32).reshape(1)
    weights = [
        lax.dynamic_slice_in_dim(weight, place * half_width, half_width)
        for place in (feat[0], 1 - feat[0])
    ]
    depth = own_blocks // SLABS
    before, new_rows = [], []
    for at, part in enumerate(incoming):
        if new_rows:
            part, other = lax.optimization_barrier((part, other))
        mine = (own[at * depth : (at + 1) * depth] + part.astype(jnp.float32)).astype(jnp.bfloat16)
        mine = mine.reshape(depth * block_size, half_width)
        other = passed_along(mine, "feat", 1)
        rows, *before = dense(
            mine,
            other,
            weights,
            bias[None],
            cotangent,
            at * depth * block_size,
            before,
            at == SLABS - 1,
        )
        new_rows.append(rows)
    grad_weight, grad_bias = summed(*before, count, feat)
    return (jnp.concatenate(new_rows), grad_weight, grad_bias[0])


def solution(mesh):
    placed = (
        P("dom", "feat"),
        P("dom", None, None),
        P("dom", None, None, None, None),
        P("dom", None, None),
        P("dom", None, None),
        P("dom", None),
        P("dom", None),
        P(None, "feat"),
        P("feat"),
        P("dom", "feat"),
    )
    return jax.shard_map(
        per_device,
        mesh=mesh,
        in_specs=placed,
        out_specs=(P("dom", "feat"), P(None, "feat"), P("feat")),
        check_vma=False,
    )
```

```python
import functools

import jax
import jax.numpy as jnp
from jax import lax
from jax.experimental import pallas as pl
from jax.experimental.pallas import tpu as pltpu
from jax.sharding import PartitionSpec as P

PEERS = 4
VMEM = pl.BlockSpec(memory_space=pltpu.VMEM)
HBM = pl.BlockSpec(memory_space=pltpu.HBM)
SMEM = pl.BlockSpec(memory_space=pltpu.SMEM)
SLABS = 2
PARAMS = pltpu.CompilerParams(vmem_limit_bytes=48 * 1024 * 1024)


def partner(block, bits):
    count = lax.axis_size("dom")
    return lax.ppermute(block, "dom", [(i, i ^ bits) for i in range(count)])


def passed_along(block, axis, distance):
    count = lax.axis_size(axis)
    return lax.ppermute(block, axis, [((i - distance) % count, i) for i in range(count)])


def select_kernel(members, cap, me_ref, *refs):
    asked, held, out = refs[: PEERS - 1], refs[PEERS - 1 : -(PEERS - 1)], refs[-(PEERS - 1) :]
    for at, member in enumerate(members):
        owner = me_ref[0] ^ (member * PEERS)
        for j in range(PEERS - 1):
            for c in range(cap):
                wanted = jnp.maximum(asked[j][c, owner], 0)
                out[j][at * cap + c] = held[at][wanted]


def select_blocks(me, asked, members, held, cap):
    size = held[0].shape[1:]
    shape = jax.ShapeDtypeStruct((len(members) * cap, *size), held[0].dtype)
    return pl.pallas_call(
        functools.partial(select_kernel, members, cap),
        out_shape=[shape] * (PEERS - 1),
        in_specs=[SMEM] * PEERS + [VMEM] * len(members),
        out_specs=[VMEM] * (PEERS - 1),
        compiler_params=PARAMS,
    )(me, *asked, *held)


def begin_kernel(chunks, *refs):
    arrays, acc, held, sems = refs[:4], refs[4], refs[5:9], refs[9]
    src_ref, dst_ref, blocks_ref, tiles_ref = held
    per_chunk = tiles_ref.shape[0] // chunks
    whole = [pltpu.make_async_copy(arrays[i], held[i], sems.at[i]) for i in range(3)]
    parts = []
    for i in range(chunks):
        rows = pl.ds(i * per_chunk, per_chunk)
        parts.append(
            pltpu.make_async_copy(arrays[3].at[rows], tiles_ref.at[rows], sems.at[3 + i])
        )
    for copy in whole + parts:
        copy.start()
    acc[...] = jnp.zeros_like(acc)
    for copy in whole:
        copy.wait()
    for i in range(chunks):
        parts[i].wait()
        for k in range(i * per_chunk, (i + 1) * per_chunk):
            product = jnp.dot(
                tiles_ref[k], blocks_ref[src_ref[0, k]], preferred_element_type=jnp.float32
            )
            dst = dst_ref[0, k]
            acc[dst] = acc[dst] + product


def begin_sum(src, dst, tiles, blocks, row_count):
    count, size, _ = tiles.shape
    chunks = 8
    return pl.pallas_call(
        functools.partial(begin_kernel, chunks),
        out_shape=[jax.ShapeDtypeStruct((row_count, size, blocks.shape[-1]), jnp.float32)],
        in_specs=[HBM] * 4,
        out_specs=[VMEM],
        scratch_shapes=[
            pltpu.SMEM(src.shape, src.dtype),
            pltpu.SMEM(dst.shape, dst.dtype),
            pltpu.VMEM(blocks.shape, blocks.dtype),
            pltpu.VMEM(tiles.shape, tiles.dtype),
            pltpu.SemaphoreType.DMA((3 + chunks,)),
        ],
        compiler_params=PARAMS,
    )(*[pltpu.with_memory_space_constraint(x, pltpu.HBM) for x in (src, dst, blocks, tiles)])


def sum_kernel(sources, cap, last, me_ref, wanted_ref, dst_ref, tiles_ref, acc_in, *refs):
    acc = refs[-1]
    acc[...] = acc_in[...]
    for bits, at, start in sources:
        owner = me_ref[0] ^ bits
        for c in range(cap):
            wanted = wanted_ref[c, owner]
            block = refs[at][jnp.maximum(wanted, 0) if start is None else start + c]
            block = jnp.where(wanted >= 0, block, jnp.zeros_like(block))
            product = jnp.dot(
                tiles_ref[owner * cap + c], block, preferred_element_type=jnp.float32
            )
            dst = dst_ref[c, owner]
            acc[dst] = acc[dst] + product
    if last:
        own_ref, *next_refs = refs[-2 - SLABS : -1]
        at = own_ref.shape[0]
        own_ref[...] = acc[:at]
        for next_ref in next_refs:
            depth = next_ref.shape[0]
            next_ref[...] = acc[at : at + depth].astype(next_ref.dtype)
            at += depth


def tile_sum(shared, acc, sources, cap, last=False):
    row_count, size, width = acc.shape
    half = (row_count // 2, size, width)
    part = (row_count // 2 // SLABS, size, width)
    arrays, places = [], []
    for bits, array, start in sources:
        known = [i for i, other in enumerate(arrays) if other is array]
        if not known:
            known = [len(arrays)]
            arrays.append(array)
        places.append((bits, known[0], start))
    scratch = []
    out_shape = [jax.ShapeDtypeStruct(acc.shape, jnp.float32)]
    if last:
        out_shape = [jax.ShapeDtypeStruct(half, jnp.float32)]
        out_shape += [jax.ShapeDtypeStruct(part, jnp.bfloat16)] * SLABS
        scratch = [pltpu.VMEM(acc.shape, jnp.float32)]
    return pl.pallas_call(
        functools.partial(sum_kernel, places, cap, last),
        out_shape=out_shape,
        in_specs=[SMEM] * 3 + [VMEM] * (2 + len(arrays)),
        out_specs=[VMEM] * len(out_shape),
        scratch_shapes=scratch,
        compiler_params=PARAMS,
    )(*shared, acc, *arrays)


def dense_kernel(start, first, last, *refs):
    mine_ref, other_ref, weight_mine, weight_other, bias_ref, cot_ref = refs[:6]
    before = [] if first else refs[6:8]
    rows_ref, weight_out, bias_out = refs[6 + len(before) : 9 + len(before)]
    depth, width = mine_ref.shape
    step = min(depth, 256)
    terms = [jnp.zeros(weight_mine.shape, jnp.float32)] * 2 if first else [
        before[0][: weight_mine.shape[0]], before[0][weight_mine.shape[0] :]
    ]
    bias_sum = jnp.zeros((1, width), jnp.float32) if first else before[1][...]
    scale = 0.7978845608028654
    cubic = 0.044715
    for at in range(0, depth, step):
        mine, other = mine_ref[at : at + step], other_ref[at : at + step]
        v = (
            jnp.dot(mine, weight_mine[...], preferred_element_type=jnp.float32)
            + jnp.dot(other, weight_other[...], preferred_element_type=jnp.float32)
            + bias_ref[...]
        )
        square = v * v
        bent = jnp.tanh(scale * v * (1.0 + cubic * square))
        half = 0.5 * (1.0 + bent)
        rows_ref[at : at + step] = (v * half).astype(rows_ref.dtype)
        slope = half + 0.5 * v * (1.0 - bent * bent) * scale * (1.0 + 3.0 * cubic * square)
        cot = cot_ref[start + at : start + at + step].astype(jnp.float32)
        grad = (cot * slope).astype(jnp.bfloat16)
        bias_sum = bias_sum + jnp.sum(grad.astype(jnp.float32), axis=0, keepdims=True)
        for i, part in enumerate((mine, other)):
            terms[i] = terms[i] + lax.dot_general(
                part, grad, (((0,), (0,)), ((), ())), preferred_element_type=jnp.float32
            )
    if last:
        sent = refs[9 + len(before)]
        at = 0
        for term in terms:
            sent[at : at + width] = term.astype(sent.dtype)
            weight_out[at : at + width] = term.astype(sent.dtype).astype(jnp.float32)
            at += width
        high = bias_sum.astype(sent.dtype).astype(jnp.float32)
        low = (bias_sum - high).astype(sent.dtype).astype(jnp.float32)
        bias_out[...] = high + low
        rows = [jnp.broadcast_to(row, (8, width)) for row in (high, low)]
        sent[at : at + 16] = jnp.concatenate(rows).astype(sent.dtype)
    else:
        weight_out[: weight_mine.shape[0]] = terms[0]
        weight_out[weight_mine.shape[0] :] = terms[1]
        bias_out[...] = bias_sum


def dense(mine, other, weights, bias, cotangent, start, before, last):
    depth, width = mine.shape
    rows = 2 * width
    out_shape = [
        jax.ShapeDtypeStruct((depth, width), jnp.bfloat16),
        jax.ShapeDtypeStruct((rows, width), jnp.float32),
        jax.ShapeDtypeStruct((1, width), jnp.float32),
    ]
    if last:
        out_shape.append(jax.ShapeDtypeStruct((rows + 16, width), jnp.bfloat16))
    return pl.pallas_call(
        functools.partial(dense_kernel, start, not before, last),
        out_shape=out_shape,
        in_specs=[VMEM] * (6 + len(before)),
        out_specs=[VMEM] * len(out_shape),
        compiler_params=PARAMS,
    )(mine, other, *weights, bias, cotangent, *before)


def rounded(value):
    return lax.reduce_precision(value, 8, 7)


def finish_kernel(feat_ref, weight_ref, bias_ref, *refs):
    *got_refs, weight_out, bias_out = refs
    depth = weight_ref.shape[0]
    half = depth // 2
    feat = feat_ref[0]

    def total(mine, start, rows):
        got = [ref[start : start + rows].astype(jnp.float32) for ref in got_refs]
        mine = mine + got[0]
        return mine + (got[1] + got[2]) if len(got) > 1 else mine

    for at, place in ((0, feat), (half, 1 - feat)):
        weight_out[pl.ds(pl.multiple_of(place * half, half), half)] = total(
            weight_ref[at : at + half], at, half
        )
    rows = [ref[depth:].astype(jnp.float32) for ref in got_refs]
    rows = [part[:1] + part[8:9] for part in rows]
    bias = bias_ref[...] + rows[0]
    bias_out[...] = bias + (rows[1] + rows[2]) if len(rows) > 1 else bias


def summed(weight_term, bias_term, sent, count, feat):
    depth, width = weight_term.shape

    def taken(raw):
        got = raw.astype(jnp.float32)
        return got[:depth], got[depth : depth + 1] + got[depth + 8 : depth + 9]

    plan, bits = [], 1
    while bits < count:
        plan.append([bits * j for j in range(1, min(PEERS, count // bits))])
        bits *= PEERS
    for at, bits in enumerate(plan):
        raw = [partner(sent, k) for k in bits]
        if at == len(plan) - 1:
            break
        got = [taken(part) for part in raw]
        weight_term, bias_term = weight_term + got[0][0], bias_term + got[0][1]
        if len(got) > 1:
            weight_term = weight_term + (got[1][0] + got[2][0])
            bias_term = bias_term + (got[1][1] + got[2][1])
        weight_term = rounded(weight_term)
        high = rounded(bias_term)
        low = rounded(bias_term - high)
        bias_term = high + low
        rows = [jnp.broadcast_to(row, (8, width)) for row in (high, low)]
        sent = jnp.concatenate([weight_term, *rows]).astype(jnp.bfloat16)
    return pl.pallas_call(
        finish_kernel,
        out_shape=[
            jax.ShapeDtypeStruct((depth, width), jnp.float32),
            jax.ShapeDtypeStruct((1, width), jnp.float32),
        ],
        in_specs=[SMEM] + [VMEM] * (2 + len(raw)),
        out_specs=[VMEM] * 2,
        compiler_params=PARAMS,
    )(feat, weight_term, bias_term, *raw)


def per_device(
    history,
    pull_list,
    remote_tiles,
    remote_dst,
    local_tiles,
    local_src,
    local_dst,
    weight,
    bias,
    cotangent,
):
    count = lax.axis_size("dom")
    columns = count // PEERS
    cap = pull_list.shape[2]
    half_width = history.shape[1]
    block_size = local_tiles.shape[1]
    own_blocks = history.shape[0] // block_size
    row_count = 2 * own_blocks
    blocks = history.reshape(own_blocks, block_size, half_width)
    me = lax.axis_index("dom").astype(jnp.int32).reshape(1)
    wanted = pull_list[0].T
    tiles = remote_tiles.reshape(-1, block_size, block_size)
    shared = (me, wanted, remote_dst[0].T, tiles)

    def exchange(members):
        picked = select_blocks(me, asked, members, [held[k] for k in members], cap)
        pulled = [partner(picked[j - 1], j) for j in range(1, PEERS)]
        sources = []
        for at, member in enumerate(members):
            sources.append((member * PEERS, held[member], None))
            for j in range(1, PEERS):
                sources.append((member * PEERS + j, pulled[j - 1], at * cap))
        return sources

    held = {0: blocks}
    for member in range(columns // 2, 0, -1):
        if member & (member - 1) == 0:
            held[member] = partner(blocks, member * PEERS)
    asked = [partner(wanted, j) for j in range(1, PEERS)]
    (acc,) = begin_sum(local_src, local_dst, local_tiles, blocks, row_count)
    for member in range(1, columns):
        if member not in held:
            low = member & -member
            source, acc, *asked = lax.optimization_barrier((held[member ^ low], acc, *asked))
            held[member] = partner(source, low * PEERS)

    first = exchange(list(range(columns - 1)))
    rest = exchange([columns - 1])
    (acc,) = tile_sum(shared, acc, first, cap)
    outs = tile_sum(shared, acc, rest, cap, last=True)
    own, *following = outs
    incoming = [passed_along(part, "dom", 1) for part in following]

    feat = lax.axis_index("feat").astype(jnp.int32).reshape(1)
    weights = [
        lax.dynamic_slice_in_dim(weight, place * half_width, half_width)
        for place in (feat[0], 1 - feat[0])
    ]
    depth = own_blocks // SLABS
    before, new_rows = [], []
    for at, part in enumerate(incoming):
        if new_rows:
            part, other = lax.optimization_barrier((part, other))
        mine = (own[at * depth : (at + 1) * depth] + part.astype(jnp.float32)).astype(jnp.bfloat16)
        mine = mine.reshape(depth * block_size, half_width)
        other = passed_along(mine, "feat", 1)
        rows, *before = dense(
            mine,
            other,
            weights,
            bias[None],
            cotangent,
            at * depth * block_size,
            before,
            at == SLABS - 1,
        )
        new_rows.append(rows)
    grad_weight, grad_bias = summed(*before, count, feat)
    return (jnp.concatenate(new_rows), grad_weight, grad_bias[0])


def solution(mesh):
    placed = (
        P("dom", "feat"),
        P("dom", None, None),
        P("dom", None, None, None, None),
        P("dom", None, None),
        P("dom", None, None),
        P("dom", None),
        P("dom", None),
        P(None, "feat"),
        P("feat"),
        P("dom", "feat"),
    )
    return jax.shard_map(
        per_device,
        mesh=mesh,
        in_specs=placed,
        out_specs=(P("dom", "feat"), P(None, "feat"), P("feat")),
        check_vma=False,
    )
```

```python
import functools

import jax
import jax.numpy as jnp
from jax import lax
from jax.experimental import pallas as pl
from jax.experimental.pallas import tpu as pltpu
from jax.sharding import PartitionSpec as P

PEERS = 4
VMEM = pl.BlockSpec(memory_space=pltpu.VMEM)
HBM = pl.BlockSpec(memory_space=pltpu.HBM)
SMEM = pl.BlockSpec(memory_space=pltpu.SMEM)
SLABS = 2
PARAMS = pltpu.CompilerParams(vmem_limit_bytes=48 * 1024 * 1024)


def partner(block, bits):
    count = lax.axis_size("dom")
    return lax.ppermute(block, "dom", [(i, i ^ bits) for i in range(count)])


def passed_along(block, axis, distance):
    count = lax.axis_size(axis)
    return lax.ppermute(block, axis, [((i - distance) % count, i) for i in range(count)])


def select_kernel(members, cap, me_ref, *refs):
    asked, held, out = refs[: PEERS - 1], refs[PEERS - 1 : -(PEERS - 1)], refs[-(PEERS - 1) :]
    for at, member in enumerate(members):
        owner = me_ref[0] ^ (member * PEERS)
        for j in range(PEERS - 1):
            for c in range(cap):
                wanted = jnp.maximum(asked[j][c, owner], 0)
                out[j][at * cap + c] = held[at][wanted]


def select_blocks(me, asked, members, held, cap):
    size = held[0].shape[1:]
    shape = jax.ShapeDtypeStruct((len(members) * cap, *size), held[0].dtype)
    return pl.pallas_call(
        functools.partial(select_kernel, members, cap),
        out_shape=[shape] * (PEERS - 1),
        in_specs=[SMEM] * PEERS + [VMEM] * len(members),
        out_specs=[VMEM] * (PEERS - 1),
        compiler_params=PARAMS,
    )(me, *asked, *held)


def begin_kernel(chunks, *refs):
    arrays, acc, held, sems = refs[:4], refs[4], refs[5:9], refs[9]
    src_ref, dst_ref, blocks_ref, tiles_ref = held
    per_chunk = tiles_ref.shape[0] // chunks
    whole = [pltpu.make_async_copy(arrays[i], held[i], sems.at[i]) for i in range(3)]
    parts = []
    for i in range(chunks):
        rows = pl.ds(i * per_chunk, per_chunk)
        parts.append(
            pltpu.make_async_copy(arrays[3].at[rows], tiles_ref.at[rows], sems.at[3 + i])
        )
    for copy in whole + parts:
        copy.start()
    acc[...] = jnp.zeros_like(acc)
    for copy in whole:
        copy.wait()
    for i in range(chunks):
        parts[i].wait()
        for k in range(i * per_chunk, (i + 1) * per_chunk):
            product = jnp.dot(
                tiles_ref[k], blocks_ref[src_ref[0, k]], preferred_element_type=jnp.float32
            )
            dst = dst_ref[0, k]
            acc[dst] = acc[dst] + product


def begin_sum(src, dst, tiles, blocks, row_count):
    count, size, _ = tiles.shape
    chunks = 8
    return pl.pallas_call(
        functools.partial(begin_kernel, chunks),
        out_shape=[jax.ShapeDtypeStruct((row_count, size, blocks.shape[-1]), jnp.float32)],
        in_specs=[HBM] * 4,
        out_specs=[VMEM],
        scratch_shapes=[
            pltpu.SMEM(src.shape, src.dtype),
            pltpu.SMEM(dst.shape, dst.dtype),
            pltpu.VMEM(blocks.shape, blocks.dtype),
            pltpu.VMEM(tiles.shape, tiles.dtype),
            pltpu.SemaphoreType.DMA((3 + chunks,)),
        ],
        compiler_params=PARAMS,
    )(*[pltpu.with_memory_space_constraint(x, pltpu.HBM) for x in (src, dst, blocks, tiles)])


def sum_kernel(sources, cap, last, me_ref, wanted_ref, dst_ref, tiles_ref, acc_in, *refs):
    acc = refs[-1]
    acc[...] = acc_in[...]
    for bits, at, start in sources:
        owner = me_ref[0] ^ bits
        for c in range(cap):
            wanted = wanted_ref[c, owner]
            block = refs[at][jnp.maximum(wanted, 0) if start is None else start + c]
            block = jnp.where(wanted >= 0, block, jnp.zeros_like(block))
            product = jnp.dot(
                tiles_ref[owner * cap + c], block, preferred_element_type=jnp.float32
            )
            dst = dst_ref[c, owner]
            acc[dst] = acc[dst] + product
    if last:
        at = acc.shape[0] // 2
        for next_ref in refs[-1 - SLABS : -1]:
            depth = next_ref.shape[0]
            next_ref[...] = acc[at : at + depth].astype(next_ref.dtype)
            at += depth


def tile_sum(shared, acc, sources, cap, last=False):
    row_count, size, width = acc.shape
    part = (row_count // 2 // SLABS, size, width)
    arrays, places = [], []
    for bits, array, start in sources:
        known = [i for i, other in enumerate(arrays) if other is array]
        if not known:
            known = [len(arrays)]
            arrays.append(array)
        places.append((bits, known[0], start))
    out_shape = [jax.ShapeDtypeStruct(acc.shape, jnp.float32)]
    if last:
        out_shape = [jax.ShapeDtypeStruct(part, jnp.bfloat16)] * SLABS + out_shape
    return pl.pallas_call(
        functools.partial(sum_kernel, places, cap, last),
        out_shape=out_shape,
        in_specs=[SMEM] * 3 + [VMEM] * (2 + len(arrays)),
        out_specs=[VMEM] * len(out_shape),
        compiler_params=PARAMS,
    )(*shared, acc, *arrays)


def dense_kernel(start, first, last, *refs):
    mine_ref, other_ref, weight_mine, weight_other, bias_ref, cot_ref = refs[:6]
    before = [] if first else refs[6:8]
    rows_ref, weight_out, bias_out = refs[6 + len(before) : 9 + len(before)]
    depth, width = mine_ref.shape
    step = min(depth, 256)
    terms = [jnp.zeros(weight_mine.shape, jnp.float32)] * 2 if first else [
        before[0][: weight_mine.shape[0]], before[0][weight_mine.shape[0] :]
    ]
    bias_sum = jnp.zeros((1, width), jnp.float32) if first else before[1][...]
    scale = 0.7978845608028654
    cubic = 0.044715
    for at in range(0, depth, step):
        mine, other = mine_ref[at : at + step], other_ref[at : at + step]
        v = (
            jnp.dot(mine, weight_mine[...], preferred_element_type=jnp.float32)
            + jnp.dot(other, weight_other[...], preferred_element_type=jnp.float32)
            + bias_ref[...]
        )
        square = v * v
        bent = jnp.tanh(scale * v * (1.0 + cubic * square))
        half = 0.5 * (1.0 + bent)
        rows_ref[at : at + step] = (v * half).astype(rows_ref.dtype)
        slope = half + 0.5 * v * (1.0 - bent * bent) * scale * (1.0 + 3.0 * cubic * square)
        cot = cot_ref[start + at : start + at + step].astype(jnp.float32)
        grad = (cot * slope).astype(jnp.bfloat16)
        bias_sum = bias_sum + jnp.sum(grad.astype(jnp.float32), axis=0, keepdims=True)
        for i, part in enumerate((mine, other)):
            terms[i] = terms[i] + lax.dot_general(
                part, grad, (((0,), (0,)), ((), ())), preferred_element_type=jnp.float32
            )
    if last:
        sent = refs[9 + len(before)]
        at = 0
        for term in terms:
            sent[at : at + width] = term.astype(sent.dtype)
            weight_out[at : at + width] = term.astype(sent.dtype).astype(jnp.float32)
            at += width
        high = bias_sum.astype(sent.dtype).astype(jnp.float32)
        low = (bias_sum - high).astype(sent.dtype).astype(jnp.float32)
        bias_out[...] = high + low
        rows = [jnp.broadcast_to(row, (8, width)) for row in (high, low)]
        sent[at : at + 16] = jnp.concatenate(rows).astype(sent.dtype)
    else:
        weight_out[: weight_mine.shape[0]] = terms[0]
        weight_out[weight_mine.shape[0] :] = terms[1]
        bias_out[...] = bias_sum


def dense(mine, other, weights, bias, cotangent, start, before, last):
    depth, width = mine.shape
    rows = 2 * width
    out_shape = [
        jax.ShapeDtypeStruct((depth, width), jnp.bfloat16),
        jax.ShapeDtypeStruct((rows, width), jnp.float32),
        jax.ShapeDtypeStruct((1, width), jnp.float32),
    ]
    if last:
        out_shape.append(jax.ShapeDtypeStruct((rows + 16, width), jnp.bfloat16))
    return pl.pallas_call(
        functools.partial(dense_kernel, start, not before, last),
        out_shape=out_shape,
        in_specs=[VMEM] * (6 + len(before)),
        out_specs=[VMEM] * len(out_shape),
        compiler_params=PARAMS,
    )(mine, other, *weights, bias, cotangent, *before)


def rounded(value):
    return lax.reduce_precision(value, 8, 7)


def finish_kernel(feat_ref, weight_ref, bias_ref, *refs):
    *got_refs, weight_out, bias_out = refs
    depth = weight_ref.shape[0]
    half = depth // 2
    feat = feat_ref[0]

    def total(mine, start, rows):
        got = [ref[start : start + rows].astype(jnp.float32) for ref in got_refs]
        mine = mine + got[0]
        return mine + (got[1] + got[2]) if len(got) > 1 else mine

    for at, place in ((0, feat), (half, 1 - feat)):
        weight_out[pl.ds(pl.multiple_of(place * half, half), half)] = total(
            weight_ref[at : at + half], at, half
        )
    rows = [ref[depth:].astype(jnp.float32) for ref in got_refs]
    rows = [part[:1] + part[8:9] for part in rows]
    bias = bias_ref[...] + rows[0]
    bias_out[...] = bias + (rows[1] + rows[2]) if len(rows) > 1 else bias


def summed(weight_term, bias_term, sent, count, feat):
    depth, width = weight_term.shape

    def taken(raw):
        got = raw.astype(jnp.float32)
        return got[:depth], got[depth : depth + 1] + got[depth + 8 : depth + 9]

    plan, bits = [], 1
    while bits < count:
        plan.append([bits * j for j in range(1, min(PEERS, count // bits))])
        bits *= PEERS
    for at, bits in enumerate(plan):
        raw = [partner(sent, k) for k in bits]
        if at == len(plan) - 1:
            break
        got = [taken(part) for part in raw]
        weight_term, bias_term = weight_term + got[0][0], bias_term + got[0][1]
        if len(got) > 1:
            weight_term = weight_term + (got[1][0] + got[2][0])
            bias_term = bias_term + (got[1][1] + got[2][1])
        weight_term = rounded(weight_term)
        high = rounded(bias_term)
        low = rounded(bias_term - high)
        bias_term = high + low
        rows = [jnp.broadcast_to(row, (8, width)) for row in (high, low)]
        sent = jnp.concatenate([weight_term, *rows]).astype(jnp.bfloat16)
    return pl.pallas_call(
        finish_kernel,
        out_shape=[
            jax.ShapeDtypeStruct((depth, width), jnp.float32),
            jax.ShapeDtypeStruct((1, width), jnp.float32),
        ],
        in_specs=[SMEM] + [VMEM] * (2 + len(raw)),
        out_specs=[VMEM] * 2,
        compiler_params=PARAMS,
    )(feat, weight_term, bias_term, *raw)


def per_device(
    history,
    pull_list,
    remote_tiles,
    remote_dst,
    local_tiles,
    local_src,
    local_dst,
    weight,
    bias,
    cotangent,
):
    count = lax.axis_size("dom")
    columns = count // PEERS
    cap = pull_list.shape[2]
    half_width = history.shape[1]
    block_size = local_tiles.shape[1]
    own_blocks = history.shape[0] // block_size
    row_count = 2 * own_blocks
    blocks = history.reshape(own_blocks, block_size, half_width)
    me = lax.axis_index("dom").astype(jnp.int32).reshape(1)
    wanted = pull_list[0].T
    tiles = remote_tiles.reshape(-1, block_size, block_size)
    shared = (me, wanted, remote_dst[0].T, tiles)

    def exchange(members):
        picked = select_blocks(me, asked, members, [held[k] for k in members], cap)
        pulled = [partner(picked[j - 1], j) for j in range(1, PEERS)]
        sources = []
        for at, member in enumerate(members):
            sources.append((member * PEERS, held[member], None))
            for j in range(1, PEERS):
                sources.append((member * PEERS + j, pulled[j - 1], at * cap))
        return sources

    held = {0: blocks}
    for member in range(columns // 2, 0, -1):
        if member & (member - 1) == 0:
            held[member] = partner(blocks, member * PEERS)
    asked = [partner(wanted, j) for j in range(1, PEERS)]
    (acc,) = begin_sum(local_src, local_dst, local_tiles, blocks, row_count)
    for member in range(1, columns):
        if member not in held:
            low = member & -member
            source, acc, *asked = lax.optimization_barrier((held[member ^ low], acc, *asked))
            held[member] = partner(source, low * PEERS)

    first = exchange(list(range(columns - 1)))
    rest = exchange([columns - 1])
    (acc,) = tile_sum(shared, acc, first, cap)
    outs = tile_sum(shared, acc, rest, cap, last=True)
    *following, own = outs
    incoming = [passed_along(part, "dom", 1) for part in following]

    feat = lax.axis_index("feat").astype(jnp.int32).reshape(1)
    weights = [
        lax.dynamic_slice_in_dim(weight, place * half_width, half_width)
        for place in (feat[0], 1 - feat[0])
    ]
    depth = own_blocks // SLABS
    before, new_rows = [], []
    for at, part in enumerate(incoming):
        if new_rows:
            part, other = lax.optimization_barrier((part, other))
        mine = (own[at * depth : (at + 1) * depth] + part.astype(jnp.float32)).astype(jnp.bfloat16)
        mine = mine.reshape(depth * block_size, half_width)
        other = passed_along(mine, "feat", 1)
        rows, *before = dense(
            mine,
            other,
            weights,
            bias[None],
            cotangent,
            at * depth * block_size,
            before,
            at == SLABS - 1,
        )
        new_rows.append(rows)
    grad_weight, grad_bias = summed(*before, count, feat)
    return (jnp.concatenate(new_rows), grad_weight, grad_bias[0])


def solution(mesh):
    placed = (
        P("dom", "feat"),
        P("dom", None, None),
        P("dom", None, None, None, None),
        P("dom", None, None),
        P("dom", None, None),
        P("dom", None),
        P("dom", None),
        P(None, "feat"),
        P("feat"),
        P("dom", "feat"),
    )
    return jax.shard_map(
        per_device,
        mesh=mesh,
        in_specs=placed,
        out_specs=(P("dom", "feat"), P(None, "feat"), P("feat")),
        check_vma=False,
    )
```
